32 devices in a mesh: groups: 2 (over y), bins: 4 (over z), blk: 4 (over x, core).
Axes of the slice: x: 2, y: 2, z: 4, core: 2. Of those that a mesh axis runs over, the one named last changes fastest.
Arguments:
- tokens: bfloat16 [32768, 1024], P(('groups', 'bins', 'blk')), parts along dimension 0, may hold values from -6 to 6
- enc_gain: float32 [1024], replicated, may hold values from 0.25 to 1.75
- enc_weight: bfloat16 [1024, 1024], replicated, may hold values from -0.1875 to 0.1875
- lengths: int32 [32, 256], P(('groups', 'bins', 'blk')), parts along dimension 0, may hold values from 1 to 16, 1024 in all within a row
- membership: int32 [8192, 1], P(('groups', 'bins', 'blk')), parts along dimension 0, may hold values from 0 to 3; in each aligned block of 256 rows (0 to 255, 256 to 511, ...) at most 80 rows name the same one
- target_keys: int32 [8192], P(('groups', 'bins', 'blk')), parts along dimension 0, may hold values from 0 to 4095, as said below
- key_weight: bfloat16 [1024, 1024], replicated, may hold values from -0.1875 to 0.1875
- value_weight: bfloat16 [1024, 1024], replicated, may hold values from -0.1875 to 0.1875
- query_weight: bfloat16 [1024, 1024], replicated, may hold values from -0.1875 to 0.1875
- out_weight: bfloat16 [1024, 1024], replicated, may hold values from -0.1875 to 0.1875
- inducing: bfloat16 [32, 1024], replicated, may hold values from -256 to 256
- score_vector: float32 [1024], replicated, may hold values from -0.1875 to 0.1875
Outputs:
- row_grads: bfloat16 [8192, 1024], P(('groups', 'bins', 'blk')), parts along dimension 0
- slate_loss: float32 [8], P(('groups', 'bins')), parts along dimension 0
The draws below stay inside these ranges and needn't reach their ends.
There are 2 independent parts, one for each index of `groups`. The reference program is written for one: setup_inputs(seed, part) draws one part's arguments, and reference() takes and returns one part's arrays. A program takes and returns all parts, laid end to end along the dimension named above; an argument that names none is the same for every part. Nothing has to cross between parts.
Inputs may be any that keep to these rules, and one draw needn't show every extreme that they name: `membership`: within the candidates of one bin, no slate holds more than 80; some slate holds exactly 80 of some bin's candidates; every slate holds some candidate. Each bin's lengths sum to 1024. `target_keys`: each key appears once.
All inputs are finite; a program needn't handle non-finite values.
Results may differ from the reference program's by a relative error of at most 0.017.
The reference program's roundings to bfloat16 on the way count: a program that leaves them out, or rounds other values in their place, can miss the bound.
Values may be sent and summed in bfloat16 or wider, within the bound.
A program may use at most 64 MiB of HBM per device.

```python
import math
import jax
import jax.numpy as jnp
import numpy as np
from jax import lax

D = 1024
HEADS = 16
HD = 64
INDUCE = 32
LMAX = 16
TOK_DEV = 1024
C_DEV = 256
CAP = 80
C_TOTAL = 4096
N_BINS = 4
N_BLK = 4


def draw_target_keys(key, part):
    shuffled = jax.random.permutation(jax.random.fold_in(key, 7001), C_TOTAL)
    return shuffled.astype(jnp.int32)


def draw_inducing(key, part):
    result = jax.random.truncated_normal(jax.random.fold_in(key, 5011), -6.0, 6.0, (INDUCE, D), jnp.float32)
    return result.astype(jnp.bfloat16)


def block_levels(rng, shape, cuts, low, largest):
    gain, own = 1.0, jax.random.fold_in(rng, 6)
    for axis_at, blocks in cuts:
        heights = jnp.exp(jax.random.uniform(jax.random.fold_in(own, axis_at), (blocks,), jnp.float32, low / len(cuts), largest / len(cuts)))
        gain = gain * jnp.repeat(heights, shape[axis_at] // blocks).reshape([-1 if axis == axis_at else 1 for axis in range(len(shape))])
    return gain


def length_profile(number_of, total, reach, skew):
    weights = [(1 << 20) // math.isqrt(standing ** skew) + 1 for standing in range(2, number_of + 1)]
    surplus, counts = total - reach - (number_of - 1), [1] * (number_of - 1)
    while surplus > 0:
        movable = [i for i in range(number_of - 1) if counts[i] < reach]
        pool, remaining = sum([weights[i] for i in movable]), surplus
        for i in movable:
            addition = min(reach - counts[i], max(1, remaining * weights[i] // pool), surplus)
            counts[i] = counts[i] + addition
            surplus = surplus - addition
    return np.array([reach] + counts)


def ragged(stream_key, count, total, most, lean):
    if count == 2:
        one = jax.random.randint(stream_key, (), max(1, total - most), min(most, total - 1) + 1)
        return jnp.stack([one, total - one])
    tallies = jnp.asarray(length_profile(count, total, most, lean), jnp.int32)
    twos = (count - 1) // 2
    source_of, receiver = tallies[1:1 + 2 * twos:2], tallies[2:2 + 2 * twos:2]
    room = jnp.minimum(source_of - 1, most - receiver)
    passed = jax.random.randint(jax.random.fold_in(stream_key, 1), (twos,), 0, 1 << 20) % (room + 1)
    tallies = tallies.at[1:1 + 2 * twos:2].set(source_of - passed).at[2:2 + 2 * twos:2].set(receiver + passed)
    return tallies[jax.random.permutation(jax.random.fold_in(stream_key, 2), count)]


def deal_out(rng, own, number, rows, count, top, limit, skew):
    order = jax.random.permutation(rng, count)
    crowded, usual = portions_of(count, rows * top, limit, skew, True), portions_of(count, rows * top, limit, skew, False)
    places = jnp.arange(count)

    def named(sizes, rotation):
        used = int((sizes > 0).sum())
        fixed = max(1, used // 4)
        shifted = fixed + (places - fixed + rotation * (used - fixed)) % max(1, count - fixed)
        return jnp.zeros((count,), jnp.int32).at[order[jnp.where(places < fixed, places, shifted)]].set(jnp.asarray(sizes, jnp.int32))

    sizes = jnp.where(number % 4 == 0, named(crowded, number // 4), named(usual, number - number // 4 - 1))
    mixed = jax.random.permutation(jax.random.fold_in(own, 3), count)
    donor, receiver = mixed[0:count // 2 * 2:2], mixed[1:count // 2 * 2:2]
    slack = jnp.minimum(sizes[donor] - 1, limit - sizes[receiver]) // 2
    slack = jnp.where((donor == order[0]) | (receiver == order[0]) | (sizes[receiver] == 0), 0, jnp.maximum(slack, 0))
    shifted = jax.random.randint(jax.random.fold_in(own, 4), (count // 2,), 0, 1 << 20) % (slack + 1)
    sizes = sizes.at[donor].add(-shifted).at[receiver].add(shifted)
    items = jnp.searchsorted(jnp.cumsum(sizes), jnp.arange(rows * top), side="right").astype(jnp.int32)
    table = items.reshape(top, rows).T
    table = table[jax.random.permutation(jax.random.fold_in(own, 1), rows)]
    rotation = jax.random.randint(jax.random.fold_in(own, 2), (rows, 1), 0, top)
    return jnp.take_along_axis(table, (jnp.arange(top)[None, :] + rotation) % top, axis=1)


def portions_of(amount, total, limit, lean, full):
    weights = [(1 << 20) // math.isqrt(rank ** lean) + 1 for rank in range(1, amount + 1)]
    largest = limit if full else min(limit, max(-(-total // amount), total * weights[0] // sum(weights)))
    least = 1 if total - largest >= amount - 1 else 0
    given, surplus = [largest] + [least] * (amount - 1), total - largest - least * (amount - 1)
    while surplus > 0:
        movable = [i for i in range(1, amount) if given[i] < largest] or [i for i in range(1, amount) if given[i] < limit]
        pool, budget = sum([weights[i] for i in movable]), surplus
        for i in movable:
            more = min(limit - given[i], max(1, budget * weights[i] // pool), surplus)
            given[i] = given[i] + more
            surplus = surplus - more
    return np.array(given)


def gaussian(key, extent, scale, limit, cuts=(), kind=jnp.bfloat16):
    values = scale * jax.random.normal(key, extent, jnp.float32)
    if cuts:
        values = values * block_levels(key, extent, cuts, -0.22, 0.18)
    return jnp.clip(values, -limit, limit).astype(kind)


def setup_inputs(seed: int = 0, part: int = 0) -> dict:
    arg_keys = jax.random.split(jax.random.key(seed), 13)
    own_keys = jax.random.split(jax.random.fold_in(arg_keys[12], part), 13)
    tokens = gaussian(own_keys[0], (N_BINS * N_BLK * TOK_DEV, D), 1.0, 6.0, ((0, 16),))
    enc_gain = jnp.clip(1.0 + 0.15 * jax.random.normal(arg_keys[1], (D,), jnp.float32), 0.25, 1.75)
    enc_weight = gaussian(arg_keys[2], (D, D), D ** -0.5, 0.1875)
    lengths = jax.vmap(lambda own: ragged(own, C_DEV, TOK_DEV, LMAX, 1))(jax.random.split(own_keys[3], (N_BINS * N_BLK))).reshape((N_BINS * N_BLK, C_DEV)).astype(jnp.int32)
    membership_keys = jax.random.split(jax.random.fold_in(own_keys[4], 1), C_TOTAL // C_DEV)
    membership_turns = jax.random.permutation(jax.random.fold_in(own_keys[4], 3), C_TOTAL // C_DEV)
    membership = jax.vmap(lambda own, number: deal_out(jax.random.fold_in(own_keys[4], 2), own, number, C_DEV, N_BINS, 1, CAP, 1))(membership_keys, membership_turns).reshape((C_TOTAL, 1))
    target_keys = draw_target_keys(jax.random.fold_in(jax.random.fold_in(arg_keys[12], part), 71), part)
    key_weight = gaussian(arg_keys[6], (D, D), D ** -0.5, 0.1875)
    value_weight = gaussian(arg_keys[7], (D, D), D ** -0.5, 0.1875)
    query_weight = gaussian(arg_keys[8], (D, D), D ** -0.5, 0.1875)
    out_weight = gaussian(arg_keys[9], (D, D), D ** -0.5, 0.1875)
    inducing = draw_inducing(jax.random.fold_in(arg_keys[12], 71), part)
    score_vector = gaussian(arg_keys[11], (D,), D ** -0.5, 0.1875, (), jnp.float32)
    return dict(tokens=tokens, enc_gain=enc_gain, enc_weight=enc_weight, lengths=lengths, membership=membership, target_keys=target_keys, key_weight=key_weight, value_weight=value_weight, query_weight=query_weight, out_weight=out_weight, inducing=inducing, score_vector=score_vector)


def doc_section(ef, dest, induced_all, query_weight, out_weight, score_vector):
    ctot = ef.shape[0]
    eb = ef.astype(jnp.bfloat16)
    quer = jnp.dot(eb, query_weight, preferred_element_type=jnp.float32).astype(jnp.bfloat16)
    hflat = induced_all.reshape(N_BINS * INDUCE, HEADS, HD).astype(jnp.float32)
    colslate = jnp.arange(N_BINS * INDUCE, dtype=jnp.int32) // INDUCE
    blocks = ctot // 512

    def one_block(item):
        qblk, dblk = item
        qf = qblk.reshape(512, HEADS, HD).astype(jnp.float32)
        scores = jnp.einsum('nhd,jhd->nhj', qf, hflat) / jnp.sqrt(jnp.float32(HD))
        mask = colslate[None, :] == dblk[:, None]
        scores = jnp.where(mask[:, None, :], scores, -1e+30)
        weights = jax.nn.softmax(scores, axis=-1).astype(jnp.bfloat16)
        mixed = jnp.einsum('nhj,jhd->nhd', weights.astype(jnp.float32), hflat)
        return mixed.reshape(512, HEADS * HD).astype(jnp.bfloat16)
    mixed = lax.map(one_block, (quer.reshape(blocks, 512, -1), dest.reshape(blocks, 512)))
    mixed = mixed.reshape(ctot, -1)
    full = ef + jnp.dot(mixed, out_weight, preferred_element_type=jnp.float32)
    return lax.optimization_barrier(jnp.sum(full * score_vector, axis=-1))

def reference(tokens, enc_gain, enc_weight, lengths, membership, target_keys, key_weight, value_weight, query_weight, out_weight, inducing, score_vector):
    xf = tokens.astype(jnp.float32)
    meansq = lax.optimization_barrier(jnp.mean(xf * xf, axis=-1, keepdims=True))
    normed = (xf * lax.rsqrt(meansq + 1e-06) * enc_gain).astype(jnp.bfloat16)
    enc_tok = (xf + jnp.dot(normed, enc_weight, preferred_element_type=jnp.float32)).astype(jnp.bfloat16)
    lens = lengths.reshape(-1)
    ctot = lens.shape[0]
    segment = jnp.repeat(jnp.arange(ctot, dtype=jnp.int32), lens, total_repeat_length=tokens.shape[0])
    sums = jax.ops.segment_sum(enc_tok.astype(jnp.float32), segment, num_segments=ctot)
    encoded = (sums / lens[:, None].astype(jnp.float32)).astype(jnp.bfloat16)
    dest = membership[:, 0]
    keys = jnp.dot(encoded, key_weight, preferred_element_type=jnp.float32).astype(jnp.bfloat16)
    values = jnp.dot(encoded, value_weight, preferred_element_type=jnp.float32).astype(jnp.bfloat16)
    k32 = keys.reshape(ctot, HEADS, HD).astype(jnp.float32)
    v32 = values.reshape(ctot, HEADS, HD).astype(jnp.float32)
    iq = inducing.reshape(INDUCE, HEADS, HD).astype(jnp.float32)

    def induce(slate):
        mask = dest == slate
        scores = jnp.einsum('ihd,nhd->hin', iq, k32) / jnp.sqrt(jnp.float32(HD))
        scores = jnp.where(mask[None, None, :], scores, -1e+30)
        top = lax.optimization_barrier(jnp.max(scores, axis=-1, keepdims=True))
        probs = jnp.where(mask[None, None, :], jnp.exp(scores - top), 0.0)
        acc = jnp.einsum('hin,nhd->hid', probs, v32) / lax.optimization_barrier(jnp.sum(probs, axis=-1))[..., None]
        return jnp.transpose(acc, (1, 0, 2)).reshape(INDUCE, HEADS * HD).astype(jnp.bfloat16)
    induced_all = lax.map(induce, jnp.arange(N_BINS, dtype=jnp.int32))
    ef = encoded.astype(jnp.float32)
    score, pull = jax.vjp(lambda rows: doc_section(rows, dest, induced_all, query_weight, out_weight, score_vector), ef)
    expo = jnp.exp(score)
    blocks = ctot // 512

    def suffix(item):
        dblk, kblk = item
        keep = (dest[None, :] == dblk[:, None]) & (target_keys[None, :] >= kblk[:, None])
        return lax.optimization_barrier(jnp.sum(jnp.where(keep, expo[None, :], 0.0), axis=1))
    den = lax.map(suffix, (dest.reshape(blocks, 512), target_keys.reshape(blocks, 512))).reshape(ctot)
    loss_rows = jnp.log(den) - score
    slate_loss = jax.ops.segment_sum(loss_rows, dest, num_segments=N_BINS)
    inverse = 1.0 / den

    def prefix(item):
        dblk, kblk = item
        keep = (dest[None, :] == dblk[:, None]) & (target_keys[None, :] <= kblk[:, None])
        return lax.optimization_barrier(jnp.sum(jnp.where(keep, inverse[None, :], 0.0), axis=1))
    acc2 = lax.map(prefix, (dest.reshape(blocks, 512), target_keys.reshape(blocks, 512))).reshape(ctot)
    score_grad = expo * acc2 - 1.0
    row_grads = pull(score_grad)[0].astype(jnp.bfloat16)
    return (row_grads, slate_loss)
```

```python
import functools

import jax
import jax.numpy as jnp
from jax import lax
from jax.experimental import pallas as pl
from jax.experimental.pallas import tpu as pltpu
from jax.sharding import PartitionSpec as P

HEADS = 16
HD = 64
INDUCE = 32


def fold_induced(carry, keys_piece, values_piece, valid_piece, inducing):
    run_max, run_sum, run_acc = carry
    count = keys_piece.shape[0]
    head_keys = keys_piece.reshape(count, HEADS, HD)
    head_vals = values_piece.reshape(count, HEADS, HD).astype(jnp.float32)
    queries = inducing.reshape(INDUCE, HEADS, HD)
    scores = jnp.einsum(
        "ihd,nhd->hin", queries, head_keys, preferred_element_type=jnp.float32
    ) / jnp.sqrt(jnp.float32(HD))
    usable = valid_piece > 0
    scores = jnp.where(usable[None, None, :], scores, -1e30)
    new_max = jnp.maximum(run_max, jnp.max(scores, axis=-1))
    probs = jnp.where(usable[None, None, :], jnp.exp(scores - new_max[..., None]), 0.0)
    new_sum = jnp.sum(probs, axis=-1)
    new_acc = jnp.einsum("hin,nhd->hid", probs, head_vals)
    return (new_max, new_sum, new_acc)


def doc_scores(rows_f, induced, query_weight, out_weight, score_vector):
    count = rows_f.shape[0]
    rows_b = rows_f.astype(jnp.bfloat16)
    quer = jnp.dot(rows_b, query_weight, preferred_element_type=jnp.float32).astype(jnp.bfloat16)
    quer = quer.reshape(count, HEADS, HD)
    head_ind = induced.reshape(INDUCE, HEADS, HD)
    scores = jnp.einsum(
        "nhd,jhd->nhj", quer, head_ind, preferred_element_type=jnp.float32
    ) / jnp.sqrt(jnp.float32(HD))
    weights = jax.nn.softmax(scores, axis=-1).astype(jnp.bfloat16)
    mixed = jnp.einsum("nhj,jhd->nhd", weights, head_ind, preferred_element_type=jnp.float32)
    mixed = mixed.reshape(count, HEADS * HD).astype(jnp.bfloat16)
    full = rows_f + jnp.dot(mixed, out_weight, preferred_element_type=jnp.float32)
    return jnp.sum(full * score_vector, axis=-1)


def local(
    tokens,
    enc_gain,
    enc_weight,
    lengths,
    membership,
    target_keys,
    key_weight,
    value_weight,
    query_weight,
    out_weight,
    inducing,
    score_vector,
):
    tok_count = tokens.shape[0]
    xf = tokens.astype(jnp.float32)
    meansq = jnp.mean(xf * xf, axis=-1, keepdims=True)
    normed = (xf * lax.rsqrt(meansq + 1e-06) * enc_gain).astype(jnp.bfloat16)
    enc_tok = (xf + jnp.dot(normed, enc_weight, preferred_element_type=jnp.float32)).astype(
        jnp.bfloat16
    )
    lens = lengths[0]
    cand = lens.shape[0]
    ends = jnp.cumsum(lens)
    starts = ends - lens
    position = jnp.arange(tok_count, dtype=jnp.int32)
    member_tok = (position[None, :] >= starts[:, None]) & (position[None, :] < ends[:, None])
    pooled = jnp.dot(member_tok.astype(jnp.bfloat16), enc_tok, preferred_element_type=jnp.float32)
    encoded = (pooled / lens[:, None].astype(jnp.float32)).astype(jnp.bfloat16)
    nbins = lax.axis_size("bins")
    slots = max(2, 5 * cand // (4 * nbins))
    total_slots = nbins * slots
    dest = membership[:, 0]
    order = jnp.arange(cand, dtype=jnp.int32)
    same_dest = (dest[:, None] == dest[None, :]) & (order[:, None] > order[None, :])
    rank = jnp.sum(same_dest.astype(jnp.int32), axis=1)
    slot_of = dest * slots + rank
    placed = jnp.arange(total_slots, dtype=jnp.int32)[:, None] == slot_of[None, :]
    placed_b = placed.astype(jnp.bfloat16)
    send_rows = jnp.dot(placed_b, encoded, preferred_element_type=jnp.float32).astype(jnp.bfloat16)
    send_tags = jnp.sum(jnp.where(placed, target_keys[None, :] + 1, 0), axis=1)
    width = encoded.shape[1]
    slate_rows = lax.all_to_all(
        send_rows.reshape(nbins, slots, width), "bins", split_axis=0, concat_axis=0, tiled=True
    ).reshape(total_slots, width)
    tags = lax.all_to_all(
        send_tags.reshape(nbins, slots), "bins", split_axis=0, concat_axis=0, tiled=True
    ).reshape(total_slots)
    valid = tags > 0
    valid_b = valid.astype(jnp.bfloat16)
    keys = jnp.dot(slate_rows, key_weight, preferred_element_type=jnp.float32).astype(jnp.bfloat16)
    values = jnp.dot(slate_rows, value_weight, preferred_element_type=jnp.float32).astype(
        jnp.bfloat16
    )
    start_state = (
        jnp.full((HEADS, INDUCE), -1e30, jnp.float32),
        jnp.zeros((HEADS, INDUCE), jnp.float32),
        jnp.zeros((HEADS, INDUCE, HD), jnp.float32),
    )
    state = fold_induced(
        start_state,
        lax.all_gather(keys, "blk", axis=0, tiled=True),
        lax.all_gather(values, "blk", axis=0, tiled=True),
        lax.all_gather(valid_b, "blk", axis=0, tiled=True),
        inducing,
    )
    induced = state[2] / state[1][..., None]
    induced = jnp.transpose(induced, (1, 0, 2)).reshape(INDUCE, HEADS * HD).astype(jnp.bfloat16)
    rows_f = slate_rows.astype(jnp.float32)
    score, pull = jax.vjp(
        lambda rows: doc_scores(rows, induced, query_weight, out_weight, score_vector), rows_f
    )
    expo = jnp.where(valid, jnp.exp(score), 0.0)
    tag_f = tags.astype(jnp.float32)
    other_tags = lax.all_gather(tag_f, "blk", axis=0, tiled=True)
    other_exp = lax.all_gather(expo, "blk", axis=0, tiled=True)
    keep = other_tags[None, :] >= tag_f[:, None]
    den = jnp.sum(jnp.where(keep, other_exp[None, :], 0.0), axis=1)
    den_safe = jnp.where(valid, den, 1.0)
    loss_rows = jnp.where(valid, jnp.log(den_safe) - score, 0.0)
    slate_loss = lax.psum(jnp.sum(loss_rows), "blk")
    inverse = jnp.where(valid, 1.0 / den_safe, 0.0)
    other_tags = lax.all_gather(tag_f, "blk", axis=0, tiled=True)
    other_inv = lax.all_gather(inverse, "blk", axis=0, tiled=True)
    keep = other_tags[None, :] <= tag_f[:, None]
    acc_inv = jnp.sum(jnp.where(keep, other_inv[None, :], 0.0), axis=1)
    score_grad = jnp.where(valid, expo * acc_inv - 1.0, 0.0)
    slot_grads = pull(score_grad)[0].astype(jnp.bfloat16)
    returned = lax.all_to_all(
        slot_grads.reshape(nbins, slots, width), "bins", split_axis=0, concat_axis=0, tiled=True
    ).reshape(total_slots, width)
    row_grads = jnp.einsum(
        "sc,sd->cd", placed_b, returned, preferred_element_type=jnp.float32
    ).astype(jnp.bfloat16)
    return (row_grads, jnp.reshape(slate_loss, (1,)))


MESH = pl.DeviceIdType.MESH
F32 = jnp.float32
BF16 = jnp.bfloat16
NEG = -1e30
NT = (((1,), (1,)), ((), ()))
TN = (((0,), (0,)), ((), ()))


def dg(a, b, dims):
    return lax.dot_general(a, b, dims, preferred_element_type=F32)


def iota(shape, axis):
    return lax.broadcasted_iota(jnp.int32, shape, axis)


def fused_kernel(
    tok_hbm, we_hbm, wk_hbm, wv_hbm, wq_hbm, wo_hbm,
    gain_ref, lens_ref, mem_ref, keys_ref, ind_ref, sv_ref,
    out_ref, loss_ref,
    tok, we, wk, wv, wq, wo, etok, pool, enc, kk, vv, qq, bias,
    sbuf, s1recv, msg, recv2, gath, ubc, prob, srow, dq, bb,
    comp_all, sc_all,
    ld_sem, cs_sem, cr_sem, ss_sem, sr_sem, s1s, s1r, s2s, s2r, ags, agr, fws, fwr,
):
    nb, nk = 4, 4
    n = nb * nk
    width = tok.shape[1]
    cand = mem_ref.shape[0]
    ntok = tok.shape[0]
    total = n * cand
    hi_rows = nb * total // 128
    chips = n // 2
    pairs = HEADS // 2
    tile = 256
    mybin, myblk = lax.axis_index("bins"), lax.axis_index("blk")
    me = mybin * nk + myblk
    core = lax.rem(myblk, 2)
    chip = me // 2

    def peer(rank):
        return {"bins": rank // nk, "blk": lax.rem(rank, nk)}

    sibling = peer(chip * 2 + 1 - core)

    barrier = pltpu.get_barrier_semaphore()
    for k in range(1, n):
        pl.semaphore_signal(barrier, inc=1, device_id=peer(lax.rem(me + k, n)), device_id_type=MESH)

    tchunks = ntok // tile
    loads = [pltpu.make_async_copy(we_hbm, we, ld_sem.at[0])]
    for k in range(tchunks):
        loads.append(
            pltpu.make_async_copy(
                tok_hbm.at[pl.ds(k * tile, tile)], tok.at[pl.ds(k * tile, tile)], ld_sem.at[5 + k]
            )
        )
    loads.append(pltpu.make_async_copy(wk_hbm, wk, ld_sem.at[1]))
    loads.append(pltpu.make_async_copy(wv_hbm, wv, ld_sem.at[2]))
    loads.append(pltpu.make_async_copy(wq_hbm, wq, ld_sem.at[3]))
    loads.append(pltpu.make_async_copy(wo_hbm, wo, ld_sem.at[4]))
    for c in loads:
        c.start()

    rr, cc = iota((cand, cand), 0), iota((cand, cand), 1)
    lens_row = lens_ref[...].astype(F32)
    ends = jnp.sum(jnp.where(cc <= rr, lens_row, 0.0), axis=1, keepdims=True)
    lens_col = jnp.sum(jnp.where(cc == rr, lens_row, 0.0), axis=1, keepdims=True)
    starts = ends - lens_col
    pos = iota((cand, ntok), 1).astype(F32)
    pool[...] = jnp.where((pos >= starts) & (pos < ends), 1.0, 0.0).astype(BF16)
    inv_len = lens_col
    slate_col = mem_ref[...].astype(F32)
    slate_row = jnp.sum(jnp.where(cc == rr, slate_col, 0.0), axis=0, keepdims=True)
    key_row = keys_ref[...].astype(F32)
    key_col = jnp.sum(jnp.where(cc == rr, key_row, 0.0), axis=1, keepdims=True)
    comp_row = (slate_row * float(total) + key_row).astype(jnp.int32)
    comp_col = (slate_col * float(total) + key_col).astype(jnp.int32)
    comp_all[me] = comp_row
    lane_slate = (iota((cand, 128), 1) // INDUCE).astype(F32)
    bias[...] = jnp.where(lane_slate == slate_col, 0.0, NEG)

    pl.semaphore_wait(barrier, n - 1)
    comp_sends = []
    for k in range(1, n):
        c = pltpu.make_async_remote_copy(
            src_ref=comp_all.at[me], dst_ref=comp_all.at[me],
            send_sem=cs_sem.at[k], recv_sem=cr_sem.at[me],
            device_id=peer(lax.rem(me + k, n)), device_id_type=MESH,
        )
        c.start()
        comp_sends.append(c)

    loads[0].wait()

    def enc_chunk(k, _):
        rows = pl.ds(pl.multiple_of(k * tile, tile), tile)
        pltpu.make_async_copy(tok_hbm.at[rows], tok.at[rows], ld_sem.at[5 + k]).wait()
        x = tok[rows, :].astype(F32)
        ms = jnp.mean(x * x, axis=-1, keepdims=True)
        normed = (x * lax.rsqrt(ms + 1e-06) * gain_ref[...]).astype(BF16)
        for j in range(width // tile):
            cols = pl.ds(j * tile, tile)
            y = tok[rows, cols].astype(F32) + jnp.dot(
                normed, we[:, cols], preferred_element_type=F32
            )
            etok[rows, cols] = y.astype(BF16)
        return 0

    lax.fori_loop(0, tchunks, enc_chunk, 0)

    def tiles(body):
        def step(j, _):
            body(pl.ds(pl.multiple_of(j * tile, tile), tile))
            return 0

        lax.fori_loop(0, width // tile, step, 0)

    def pool_tile(cols):
        y = jnp.dot(pool[...], etok[:, cols], preferred_element_type=F32)
        enc[:, cols] = (y / inv_len).astype(BF16)

    tiles(pool_tile)

    def project(w, dst):
        def body(cols):
            dst[:, cols] = jnp.dot(enc[...], w[:, cols], preferred_element_type=F32).astype(BF16)

        tiles(body)

    loads[1 + tchunks].wait()
    project(wk, kk)
    loads[2 + tchunks].wait()
    project(wv, vv)

    row8 = iota((8, 128), 0)
    half_lane = iota((INDUCE, 128), 1) < HD

    def s1_copy(p):
        return pltpu.make_async_remote_copy(
            src_ref=sbuf.at[1 - core, p], dst_ref=s1recv.at[p],
            send_sem=s1s.at[p], recv_sem=s1r.at[p],
            device_id=sibling, device_id_type=MESH,
        )

    def partial_pair(p, _):
        lanes = pl.ds(pl.multiple_of(p * 128, 128), 128)
        ind = ind_ref[:, lanes].astype(F32)
        ia = jnp.where(half_lane, ind, 0.0)
        ib = jnp.where(half_lane, 0.0, ind)
        bd = jnp.concatenate([ia] * nb + [ib] * nb, axis=0).astype(BF16)
        s = dg(kk[:, lanes], bd, NT) * 0.125
        b = bias[...]
        s = s + jnp.concatenate([b, b], axis=1)
        top = jnp.maximum(jnp.max(s, axis=0, keepdims=True), -1e29)
        thi = top.astype(BF16).astype(F32)
        top = thi + (top - thi).astype(BF16).astype(F32)
        pr = jnp.exp(s - top)
        l = jnp.sum(pr, axis=0, keepdims=True)
        acc = dg(vv[:, lanes], pr.astype(BF16), TN)
        for h in range(2):
            hc = slice(h * 128, (h + 1) * 128)
            sbuf[h, p, 0:HD] = acc[h * HD:(h + 1) * HD, hc]
            sbuf[h, p, HD:HD + 8] = jnp.where(
                row8 == 0, top[:, hc], jnp.where(row8 == 1, l[:, hc], 0.0)
            )
        s1_copy(p).start()
        return 0

    lax.fori_loop(0, pairs, partial_pair, 0)

    row16 = iota((16, 128), 0)

    def s2_copy(k):
        p = lax.rem(chip + k, chips)
        return pltpu.make_async_remote_copy(
            src_ref=msg.at[p], dst_ref=recv2.at[chip],
            send_sem=s2s.at[p], recv_sem=s2r.at[chip],
            device_id=peer(p * 2 + core), device_id_type=MESH,
        )

    def merge_pair(k):
        p = lax.rem(chip + k, chips)
        s1_copy(p).wait_recv()
        m0, m1 = sbuf[core, p, HD:HD + 1], s1recv[p, HD:HD + 1]
        l0, l1 = sbuf[core, p, HD + 1:HD + 2], s1recv[p, HD + 1:HD + 2]
        mx = jnp.maximum(m0, m1)
        f0, f1 = jnp.exp(m0 - mx), jnp.exp(m1 - mx)
        l = l0 * f0 + l1 * f1
        msg[p, 0:HD] = (sbuf[core, p, 0:HD] * f0 + s1recv[p, 0:HD] * f1).astype(BF16)
        mhi = mx.astype(BF16).astype(F32)
        lhi = l.astype(BF16).astype(F32)
        st = jnp.where(row16 == 0, mhi, jnp.where(row16 == 1, mx - mhi, 0.0))
        st = jnp.where(row16 == 2, lhi, jnp.where(row16 == 3, l - lhi, st))
        msg[p, HD:HD + 16] = st.astype(BF16)

    def merge_send(k, _):
        merge_pair(k)
        s2_copy(k).start()
        return 0

    lax.fori_loop(1, chips, merge_send, 0)
    merge_pair(0)

    loads[3 + tchunks].wait()
    project(wq, qq)
    loads[4 + tchunks].wait()

    def u_tile(j, _):
        rows = pl.ds(pl.multiple_of(j * 128, 128), 128)
        a = jnp.zeros((128, 128), F32)
        for c in range(width // 128):
            cs = slice(c * 128, (c + 1) * 128)
            a = a + wo[rows, cs].astype(F32) * sv_ref[:, cs]
        ubc[rows, :] = jnp.broadcast_to(jnp.sum(a, axis=1, keepdims=True), (128, 128))
        return 0

    lax.fori_loop(0, width // 128, u_tile, 0)
    esv = jnp.sum(enc[...].astype(F32) * sv_ref[...], axis=1, keepdims=True)
    esv_row = jnp.sum(jnp.where(cc == rr, esv, 0.0), axis=0, keepdims=True)

    def s2_wait(k, _):
        src = lax.rem(chip + k, chips)
        pltpu.make_async_remote_copy(
            src_ref=msg.at[src], dst_ref=recv2.at[src],
            send_sem=s2s.at[src], recv_sem=s2r.at[src],
            device_id=sibling, device_id_type=MESH,
        ).wait_recv()
        return 0

    lax.fori_loop(1, chips, s2_wait, 0)
    recv2[chip] = msg[chip]

    def stats(i):
        st = recv2[i, HD:HD + 16].astype(F32)
        return st[0:1] + st[1:2], st[2:3] + st[3:4]

    ml = [stats(i) for i in range(chips)]
    mx = functools.reduce(jnp.maximum, [m for m, _ in ml])
    acc = jnp.zeros((HD, 128), F32)
    lsum = jnp.zeros((1, 128), F32)
    for i in range(chips):
        f = jnp.exp(ml[i][0] - mx)
        lsum = lsum + ml[i][1] * f
        acc = acc + recv2[i, 0:HD].astype(F32) * f
    gath[chip, core] = (acc / lsum).astype(BF16)

    def ag_copy(k):
        return pltpu.make_async_remote_copy(
            src_ref=gath.at[chip, core], dst_ref=gath.at[chip, core],
            send_sem=ags.at[k], recv_sem=agr.at[chip],
            device_id=peer(lax.rem(chip + k, chips) * 2 + core), device_id_type=MESH,
        )

    def fw_copy(p):
        return pltpu.make_async_remote_copy(
            src_ref=gath.at[p, core], dst_ref=gath.at[p, core],
            send_sem=fws.at[p], recv_sem=fwr.at[p],
            device_id=sibling, device_id_type=MESH,
        )

    for k in range(1, chips):
        ag_copy(k).start()
    fw_copy(chip).start()

    def comp_wait(k, _):
        src = lax.rem(me + k, n)
        pltpu.make_async_remote_copy(
            src_ref=comp_all.at[src], dst_ref=comp_all.at[src],
            send_sem=cs_sem.at[k], recv_sem=cr_sem.at[src],
            device_id=sibling, device_id_type=MESH,
        ).wait_recv()
        return 0

    lax.fori_loop(1, n, comp_wait, 0)
    hrow = iota((hi_rows, cand), 0)
    lrow = iota((128, cand), 0)

    def onehots(b):
        cr = comp_all[b]
        return (cr // 128) == hrow, jnp.where(lax.rem(cr, 128) == lrow, 1.0, 0.0).astype(BF16)

    def valid_step(b, t):
        lm, rm = onehots(b)
        return t + dg(jnp.where(lm, 1.0, 0.0).astype(BF16), rm, NT)

    valid = lax.fori_loop(0, n, valid_step, jnp.zeros((hi_rows, 128), F32))

    def forward_block(k, _):
        src = lax.rem(chip + k, chips)
        pltpu.make_async_remote_copy(
            src_ref=gath.at[src, core], dst_ref=gath.at[src, core],
            send_sem=ags.at[k], recv_sem=agr.at[src],
            device_id=sibling, device_id_type=MESH,
        ).wait_recv()
        fw_copy(src).start()
        return 0

    lax.fori_loop(1, chips, forward_block, 0)

    def fw_wait(p, _):
        pltpu.make_async_remote_copy(
            src_ref=gath.at[p, 1 - core], dst_ref=gath.at[p, 1 - core],
            send_sem=fws.at[p], recv_sem=fwr.at[p],
            device_id=sibling, device_id_type=MESH,
        ).wait_recv()
        return 0

    lax.fori_loop(0, chips, fw_wait, 0)

    masks = [slate_row == float(s) for s in range(nb)]
    half_row = iota((128, 128), 0) < HD

    def block_diag(p):
        g = jnp.concatenate([gath[p, 0], gath[p, 1]], axis=0).astype(F32)
        return jnp.concatenate(
            [jnp.where(half_row, g, 0.0), jnp.where(half_row, 0.0, g)], axis=1
        ).astype(BF16)

    def pick(z):
        r = z[0:INDUCE]
        for s in range(1, nb):
            r = jnp.where(masks[s], z[s * INDUCE:(s + 1) * INDUCE], r)
        return r

    def spread(a, b):
        return jnp.concatenate(
            [jnp.where(m, a, 0.0) for m in masks] + [jnp.where(m, b, 0.0) for m in masks], axis=0
        ).astype(BF16)

    def wide(x):
        return jnp.concatenate([x] * (cand // 128), axis=1)

    def score_pair(p, row):
        lanes = pl.ds(pl.multiple_of(p * 128, 128), 128)
        bd = block_diag(p)
        z = dg(bd, qq[:, lanes], (((0,), (1,)), ((), ())))
        ws = []
        for h in range(2):
            zs = pick(z[h * 128:(h + 1) * 128]) * 0.125
            e = jnp.exp(zs - jnp.max(zs, axis=0, keepdims=True))
            w = e / jnp.sum(e, axis=0, keepdims=True)
            prob[p, h * INDUCE:(h + 1) * INDUCE] = w
            ws.append(w)
        mix = jnp.dot(bd, spread(ws[0], ws[1]), preferred_element_type=F32)
        u = wide(ubc[lanes, :])
        mu = mix * u
        sa = jnp.sum(mu[0:HD], axis=0, keepdims=True)
        sb = jnp.sum(mu[HD:2 * HD], axis=0, keepdims=True)
        r8 = iota((8, cand), 0)
        srow[p] = jnp.where(r8 == 0, sa, sb)
        return row + jnp.sum(mix.astype(BF16).astype(F32) * u, axis=0, keepdims=True)

    score_row = lax.fori_loop(0, pairs, score_pair, esv_row)
    sc_all[me] = score_row
    sc_sends = []
    for k in range(1, n):
        c = pltpu.make_async_remote_copy(
            src_ref=sc_all.at[me], dst_ref=sc_all.at[me],
            send_sem=ss_sem.at[k], recv_sem=sr_sem.at[me],
            device_id=peer(lax.rem(me + k, n)), device_id_type=MESH,
        )
        c.start()
        sc_sends.append(c)

    def back_pair(p, _):
        lanes = pl.ds(pl.multiple_of(p * 128, 128), 128)
        bd = block_diag(p)
        u = ubc[lanes, :]
        uh = u.astype(BF16)
        ul = (u - uh.astype(F32)).astype(BF16)
        t = wide(dg(bd, uh, TN) + dg(bd, ul, TN))
        ds = []
        for h in range(2):
            ts = pick(t[h * 128:(h + 1) * 128])
            ds.append(prob[p, h * INDUCE:(h + 1) * INDUCE] * (ts - srow[p, h:h + 1]) * 0.125)
        dq[lanes, :] = jnp.dot(bd, spread(ds[0], ds[1]), preferred_element_type=F32).astype(BF16)
        return 0

    lax.fori_loop(0, pairs, back_pair, 0)

    def b_tile(cols):
        y = jnp.dot(wq[cols, :], dq[...], preferred_element_type=F32)
        bb[:, cols] = jnp.transpose(y) + sv_ref[:, cols]

    tiles(b_tile)

    def sc_wait(k, _):
        src = lax.rem(me + k, n)
        pltpu.make_async_remote_copy(
            src_ref=sc_all.at[src], dst_ref=sc_all.at[src],
            send_sem=ss_sem.at[k], recv_sem=sr_sem.at[src],
            device_id=sibling, device_id_type=MESH,
        ).wait_recv()
        return 0

    lax.fori_loop(1, n, sc_wait, 0)

    def place(b, carry):
        t, ssum = carry
        lm, rm = onehots(b)
        sc = sc_all[b]
        e = jnp.exp(sc)
        eh = e.astype(BF16).astype(F32)
        both = jnp.concatenate([jnp.where(lm, eh, 0.0), jnp.where(lm, e - eh, 0.0)], axis=0)
        y = dg(both.astype(BF16), rm, NT)
        mine = (comp_all[b] // total) == mybin
        return t + y[0:hi_rows] + y[hi_rows:], ssum + jnp.where(mine, sc, 0.0)

    table, ssum = lax.fori_loop(
        0, n, place, (jnp.zeros((hi_rows, 128), F32), jnp.zeros((1, cand), F32))
    )

    ri, ci = iota((128, 128), 0), iota((128, 128), 1)
    per = hi_rows // nb
    same = (ri // per) == (ci // per)

    def hdot(a, b):
        return jnp.dot(a, b, preferred_element_type=F32, precision=lax.Precision.HIGHEST)

    suf = jnp.where(ri >= ci, 1.0, 0.0)
    pre = jnp.where(ri <= ci, 1.0, 0.0)
    later = jnp.where(same & (ci > ri), 1.0, 0.0)
    earlier = jnp.where(same & (ci < ri), 1.0, 0.0)

    def total_of(x):
        return jnp.broadcast_to(jnp.sum(x, axis=1, keepdims=True), (hi_rows, 128))

    den = hdot(table, suf) + hdot(later, total_of(table))
    is_valid = valid > 0.5
    den = jnp.where(is_valid, den, 1.0)
    ln = jnp.where(is_valid & ((ri // per) == mybin), jnp.log(den), 0.0)
    loss_ref[0] = jnp.sum(ln) - jnp.sum(ssum)
    inv = jnp.where(is_valid, 1.0 / den, 0.0)
    acc2 = hdot(inv, pre) + hdot(earlier, total_of(inv))
    lc = jnp.where((comp_col // 128) == iota((cand, hi_rows), 1), 1.0, 0.0)
    mine = hdot(lc, acc2)
    mine = jnp.where(lax.rem(comp_col, 128) == iota((cand, 128), 1), mine, 0.0)
    acc_col = jnp.sum(mine, axis=1, keepdims=True)
    e_col = jnp.exp(jnp.sum(jnp.where(cc == rr, score_row, 0.0), axis=1, keepdims=True))
    g = e_col * acc_col - 1.0
    out_ref[...] = (bb[...] * g).astype(BF16)

    for c in comp_sends + sc_sends:
        c.wait_send()
    for p in range(pairs):
        s1_copy(p).wait_send()
        fw_copy(p).wait_send()
    for k in range(1, chips):
        s2_copy(k).wait_send()
        ag_copy(k).wait_send()


def fused(
    tokens, enc_gain, enc_weight, lengths, membership, target_keys,
    key_weight, value_weight, query_weight, out_weight, inducing, score_vector,
):
    ntok, width = tokens.shape
    cand = membership.shape[0]
    n = 16
    any_spec = pl.BlockSpec(memory_space=pl.ANY)
    vm = pl.BlockSpec(memory_space=pltpu.VMEM)
    dma = pltpu.SemaphoreType.DMA
    mat = pltpu.VMEM((width, width), BF16)
    rows = pltpu.VMEM((cand, width), BF16)
    out, loss = pl.pallas_call(
        fused_kernel,
        out_shape=(
            jax.ShapeDtypeStruct((cand, width), BF16),
            jax.ShapeDtypeStruct((1,), F32),
        ),
        in_specs=[any_spec] * 6 + [vm] * 6,
        out_specs=(vm, pl.BlockSpec(memory_space=pltpu.SMEM)),
        scratch_shapes=[
            pltpu.VMEM((ntok, width), BF16), mat, mat, mat, mat, mat,
            pltpu.VMEM((ntok, width), BF16), pltpu.VMEM((cand, ntok), BF16),
            rows, rows, rows, rows, pltpu.VMEM((cand, 128), F32),
            pltpu.VMEM((2, 8, HD + 8, 128), F32), pltpu.VMEM((8, HD + 8, 128), F32),
            pltpu.VMEM((8, HD + 16, 128), BF16), pltpu.VMEM((8, HD + 16, 128), BF16),
            pltpu.VMEM((8, 2, HD, 128), BF16), pltpu.VMEM((width, 128), F32),
            pltpu.VMEM((8, 2 * INDUCE, cand), F32), pltpu.VMEM((8, 8, cand), F32),
            pltpu.VMEM((width, cand), BF16), pltpu.VMEM((cand, width), F32),
            pltpu.VMEM((n, 1, cand), jnp.int32), pltpu.VMEM((n, 1, cand), F32),
            dma((5 + ntok // 256,)), dma((n,)), dma((n,)), dma((n,)), dma((n,)),
            dma((8,)), dma((8,)), dma((8,)), dma((8,)), dma((8,)), dma((8,)), dma((8,)), dma((8,)),
        ],
        compiler_params=pltpu.CompilerParams(
            collective_id=0, has_side_effects=True, vmem_limit_bytes=56 * 1024 * 1024
        ),
        cost_estimate=pl.CostEstimate(
            flops=8_000_000_000, bytes_accessed=13_000_000, transcendentals=1_000_000
        ),
    )(
        tokens, enc_weight, key_weight, value_weight, query_weight, out_weight,
        enc_gain.reshape(1, width), lengths, membership, target_keys.reshape(1, cand),
        inducing, score_vector.reshape(1, width),
    )
    return out, loss


def solution(mesh):
    placed = (
        P(("groups", "bins", "blk"), None),
        P(),
        P(),
        P(("groups", "bins", "blk"), None),
        P(("groups", "bins", "blk"), None),
        P(("groups", "bins", "blk")),
        P(),
        P(),
        P(),
        P(),
        P(),
        P(),
    )
    small = mesh.shape["bins"] == 4 and mesh.shape["blk"] == 4
    return jax.shard_map(
        fused if small else local,
        mesh=mesh,
        in_specs=placed,
        out_specs=(P(("groups", "bins", "blk"), None), P(("groups", "bins"))),
        check_vma=False,
    )
```

```python
import functools

import jax
import jax.numpy as jnp
from jax import lax
from jax.experimental import pallas as pl
from jax.experimental.pallas import tpu as pltpu
from jax.sharding import PartitionSpec as P

HEADS = 16
HD = 64
INDUCE = 32


def fold_induced(carry, keys_piece, values_piece, valid_piece, inducing):
    run_max, run_sum, run_acc = carry
    count = keys_piece.shape[0]
    head_keys = keys_piece.reshape(count, HEADS, HD)
    head_vals = values_piece.reshape(count, HEADS, HD).astype(jnp.float32)
    queries = inducing.reshape(INDUCE, HEADS, HD)
    scores = jnp.einsum(
        "ihd,nhd->hin", queries, head_keys, preferred_element_type=jnp.float32
    ) / jnp.sqrt(jnp.float32(HD))
    usable = valid_piece > 0
    scores = jnp.where(usable[None, None, :], scores, -1e30)
    new_max = jnp.maximum(run_max, jnp.max(scores, axis=-1))
    probs = jnp.where(usable[None, None, :], jnp.exp(scores - new_max[..., None]), 0.0)
    new_sum = jnp.sum(probs, axis=-1)
    new_acc = jnp.einsum("hin,nhd->hid", probs, head_vals)
    return (new_max, new_sum, new_acc)


def doc_scores(rows_f, induced, query_weight, out_weight, score_vector):
    count = rows_f.shape[0]
    rows_b = rows_f.astype(jnp.bfloat16)
    quer = jnp.dot(rows_b, query_weight, preferred_element_type=jnp.float32).astype(jnp.bfloat16)
    quer = quer.reshape(count, HEADS, HD)
    head_ind = induced.reshape(INDUCE, HEADS, HD)
    scores = jnp.einsum(
        "nhd,jhd->nhj", quer, head_ind, preferred_element_type=jnp.float32
    ) / jnp.sqrt(jnp.float32(HD))
    weights = jax.nn.softmax(scores, axis=-1).astype(jnp.bfloat16)
    mixed = jnp.einsum("nhj,jhd->nhd", weights, head_ind, preferred_element_type=jnp.float32)
    mixed = mixed.reshape(count, HEADS * HD).astype(jnp.bfloat16)
    full = rows_f + jnp.dot(mixed, out_weight, preferred_element_type=jnp.float32)
    return jnp.sum(full * score_vector, axis=-1)


def local(
    tokens,
    enc_gain,
    enc_weight,
    lengths,
    membership,
    target_keys,
    key_weight,
    value_weight,
    query_weight,
    out_weight,
    inducing,
    score_vector,
):
    tok_count = tokens.shape[0]
    xf = tokens.astype(jnp.float32)
    meansq = jnp.mean(xf * xf, axis=-1, keepdims=True)
    normed = (xf * lax.rsqrt(meansq + 1e-06) * enc_gain).astype(jnp.bfloat16)
    enc_tok = (xf + jnp.dot(normed, enc_weight, preferred_element_type=jnp.float32)).astype(
        jnp.bfloat16
    )
    lens = lengths[0]
    cand = lens.shape[0]
    seq = jnp.arange(cand, dtype=jnp.int32)
    ends = jnp.sum(jnp.where(seq[None, :] <= seq[:, None], lens[None, :], 0), axis=1)
    starts = ends - lens
    position = jnp.arange(tok_count, dtype=jnp.int32)
    member_tok = (position[None, :] >= starts[:, None]) & (position[None, :] < ends[:, None])
    pooled = jnp.dot(member_tok.astype(jnp.bfloat16), enc_tok, preferred_element_type=jnp.float32)
    encoded = (pooled / lens[:, None].astype(jnp.float32)).astype(jnp.bfloat16)
    nbins = lax.axis_size("bins")
    slots = max(2, 5 * cand // (4 * nbins))
    total_slots = nbins * slots
    dest = membership[:, 0]
    order = jnp.arange(cand, dtype=jnp.int32)
    same_dest = (dest[:, None] == dest[None, :]) & (order[:, None] > order[None, :])
    rank = jnp.sum(same_dest.astype(jnp.int32), axis=1)
    slot_of = dest * slots + rank
    placed = jnp.arange(total_slots, dtype=jnp.int32)[:, None] == slot_of[None, :]
    placed_b = placed.astype(jnp.bfloat16)
    send_rows = jnp.dot(placed_b, encoded, preferred_element_type=jnp.float32).astype(jnp.bfloat16)
    send_tags = jnp.sum(jnp.where(placed, target_keys[None, :] + 1, 0), axis=1)
    width = encoded.shape[1]
    slate_rows = lax.all_to_all(
        send_rows.reshape(nbins, slots, width), "bins", split_axis=0, concat_axis=0, tiled=True
    ).reshape(total_slots, width)
    tags = lax.all_to_all(
        send_tags.reshape(nbins, slots), "bins", split_axis=0, concat_axis=0, tiled=True
    ).reshape(total_slots)
    valid = tags > 0
    valid_b = valid.astype(jnp.bfloat16)
    keys = jnp.dot(slate_rows, key_weight, preferred_element_type=jnp.float32).astype(jnp.bfloat16)
    values = jnp.dot(slate_rows, value_weight, preferred_element_type=jnp.float32).astype(
        jnp.bfloat16
    )
    start_state = (
        jnp.full((HEADS, INDUCE), -1e30, jnp.float32),
        jnp.zeros((HEADS, INDUCE), jnp.float32),
        jnp.zeros((HEADS, INDUCE, HD), jnp.float32),
    )
    state = fold_induced(
        start_state,
        lax.all_gather(keys, "blk", axis=0, tiled=True),
        lax.all_gather(values, "blk", axis=0, tiled=True),
        lax.all_gather(valid_b, "blk", axis=0, tiled=True),
        inducing,
    )
    induced = state[2] / state[1][..., None]
    induced = jnp.transpose(induced, (1, 0, 2)).reshape(INDUCE, HEADS * HD).astype(jnp.bfloat16)
    rows_f = slate_rows.astype(jnp.float32)
    score, pull = jax.vjp(
        lambda rows: doc_scores(rows, induced, query_weight, out_weight, score_vector), rows_f
    )
    expo = jnp.where(valid, jnp.exp(score), 0.0)
    tag_f = tags.astype(jnp.float32)
    other_tags = lax.all_gather(tag_f, "blk", axis=0, tiled=True)
    other_exp = lax.all_gather(expo, "blk", axis=0, tiled=True)
    keep = other_tags[None, :] >= tag_f[:, None]
    den = jnp.sum(jnp.where(keep, other_exp[None, :], 0.0), axis=1)
    den_safe = jnp.where(valid, den, 1.0)
    loss_rows = jnp.where(valid, jnp.log(den_safe) - score, 0.0)
    slate_loss = lax.psum(jnp.sum(loss_rows), "blk")
    inverse = jnp.where(valid, 1.0 / den_safe, 0.0)
    other_tags = lax.all_gather(tag_f, "blk", axis=0, tiled=True)
    other_inv = lax.all_gather(inverse, "blk", axis=0, tiled=True)
    keep = other_tags[None, :] <= tag_f[:, None]
    acc_inv = jnp.sum(jnp.where(keep, other_inv[None, :], 0.0), axis=1)
    score_grad = jnp.where(valid, expo * acc_inv - 1.0, 0.0)
    slot_grads = pull(score_grad)[0].astype(jnp.bfloat16)
    returned = lax.all_to_all(
        slot_grads.reshape(nbins, slots, width), "bins", split_axis=0, concat_axis=0, tiled=True
    ).reshape(total_slots, width)
    row_grads = jnp.einsum(
        "sc,sd->cd", placed_b, returned, preferred_element_type=jnp.float32
    ).astype(jnp.bfloat16)
    return (row_grads, jnp.reshape(slate_loss, (1,)))


MESH = pl.DeviceIdType.MESH
F32 = jnp.float32
BF16 = jnp.bfloat16
NEG = -1e30
NT = (((1,), (1,)), ((), ()))
TN = (((0,), (0,)), ((), ()))


def dg(a, b, dims):
    return lax.dot_general(a, b, dims, preferred_element_type=F32)


def iota(shape, axis):
    return lax.broadcasted_iota(jnp.int32, shape, axis)


def fused_kernel(
    tok_hbm, we_hbm, wk_hbm, wv_hbm, wq_hbm, wo_hbm,
    gain_ref, lens_ref, mem_ref, keys_ref, ind_ref, sv_ref,
    bb_hbm, g_ref, loss_ref,
    tok, we, wk, wv, wq, wo, etok, pool, enc, kk, vv, qq, bias,
    sbuf, s1recv, msg, recv2, gath, ubc, prob, srow, dq, bb,
    comp_all, sc_all,
    ld_sem, cs_sem, cr_sem, ss_sem, sr_sem, s1s, s1r, s2s, s2r, ags, agr, fws, fwr,
    out_sem, rt,
):
    nb, nk = 4, 4
    n = nb * nk
    width = tok.shape[1]
    cand = mem_ref.shape[1]
    ntok = tok.shape[0]
    total = n * cand
    hi_rows = nb * total // 128
    chips = n // 2
    pairs = HEADS // 2
    tile = 256
    mybin, myblk = lax.axis_index("bins"), lax.axis_index("blk")
    me = mybin * nk + myblk
    core = lax.rem(myblk, 2)
    chip = me // 2

    def peer(rank):
        return {"bins": rank // nk, "blk": lax.rem(rank, nk)}

    sibling = peer(chip * 2 + 1 - core)

    barrier = pltpu.get_barrier_semaphore()
    for k in range(1, n):
        pl.semaphore_signal(barrier, inc=1, device_id=peer(lax.rem(me + k, n)), device_id_type=MESH)

    tchunks = ntok // tile
    loads = [pltpu.make_async_copy(we_hbm, we, ld_sem.at[0])]
    for k in range(tchunks):
        loads.append(
            pltpu.make_async_copy(
                tok_hbm.at[pl.ds(k * tile, tile)], tok.at[pl.ds(k * tile, tile)], ld_sem.at[5 + k]
            )
        )
    loads.append(pltpu.make_async_copy(wk_hbm, wk, ld_sem.at[1]))
    loads.append(pltpu.make_async_copy(wv_hbm, wv, ld_sem.at[2]))
    loads.append(pltpu.make_async_copy(wq_hbm, wq, ld_sem.at[3]))
    loads.append(pltpu.make_async_copy(wo_hbm, wo, ld_sem.at[4]))
    for c in loads[: 1 + tchunks]:
        c.start()

    rr, cc = iota((cand, cand), 0), iota((cand, cand), 1)
    lens_row = lens_ref[...].astype(F32)
    ends = jnp.sum(jnp.where(cc <= rr, lens_row, 0.0), axis=1, keepdims=True)
    lens_col = jnp.sum(jnp.where(cc == rr, lens_row, 0.0), axis=1, keepdims=True)
    starts = ends - lens_col
    pos = iota((cand, ntok), 1).astype(F32)
    pool[...] = jnp.where((pos >= starts) & (pos < ends), 1.0, 0.0).astype(BF16)
    inv_len = lens_col
    slate_row = mem_ref[...].astype(F32)
    slate_col = jnp.sum(jnp.where(cc == rr, slate_row, 0.0), axis=1, keepdims=True)
    key_row = keys_ref[...].astype(F32)
    key_col = jnp.sum(jnp.where(cc == rr, key_row, 0.0), axis=1, keepdims=True)
    comp_row = (slate_row * float(total) + key_row).astype(jnp.int32)
    comp_col = (slate_col * float(total) + key_col).astype(jnp.int32)
    comp_all[me] = comp_row
    lane_slate = (iota((cand, 128), 1) // INDUCE).astype(F32)
    bias[...] = jnp.where(lane_slate == slate_col, 0.0, NEG)

    pl.semaphore_wait(barrier, n - 1)
    comp_sends = []
    for k in range(1, n):
        c = pltpu.make_async_remote_copy(
            src_ref=comp_all.at[me], dst_ref=comp_all.at[me],
            send_sem=cs_sem.at[k], recv_sem=cr_sem.at[me],
            device_id=peer(lax.rem(me + k, n)), device_id_type=MESH,
        )
        c.start()
        comp_sends.append(c)

    loads[0].wait()
    loads[1 + tchunks].start()
    loads[2 + tchunks].start()

    def enc_chunk(k, _):
        rows = pl.ds(pl.multiple_of(k * tile, tile), tile)
        pltpu.make_async_copy(tok_hbm.at[rows], tok.at[rows], ld_sem.at[5 + k]).wait()
        x = tok[rows, :].astype(F32)
        ms = jnp.mean(x * x, axis=-1, keepdims=True)
        normed = (x * lax.rsqrt(ms + 1e-06) * gain_ref[...]).astype(BF16)
        for j in range(width // tile):
            cols = pl.ds(j * tile, tile)
            y = tok[rows, cols].astype(F32) + jnp.dot(
                normed, we[:, cols], preferred_element_type=F32
            )
            etok[rows, cols] = y.astype(BF16)
        return 0

    lax.fori_loop(0, tchunks, enc_chunk, 0)
    loads[3 + tchunks].start()
    loads[4 + tchunks].start()

    def tiles(body):
        def step(j, _):
            body(pl.ds(pl.multiple_of(j * tile, tile), tile))
            return 0

        lax.fori_loop(0, width // tile, step, 0)

    def pool_tile(cols):
        y = jnp.dot(pool[...], etok[:, cols], preferred_element_type=F32)
        enc[:, cols] = (y / inv_len).astype(BF16)

    tiles(pool_tile)

    def project(w, dst):
        def body(cols):
            dst[:, cols] = jnp.dot(enc[...], w[:, cols], preferred_element_type=F32).astype(BF16)

        tiles(body)

    loads[1 + tchunks].wait()
    project(wk, kk)
    loads[2 + tchunks].wait()
    project(wv, vv)

    row8 = iota((8, 128), 0)
    half_lane = iota((INDUCE, 128), 1) < HD

    def s1_copy(p):
        return pltpu.make_async_remote_copy(
            src_ref=sbuf.at[1 - core, p], dst_ref=s1recv.at[p],
            send_sem=s1s.at[p], recv_sem=s1r.at[p],
            device_id=sibling, device_id_type=MESH,
        )

    def partial_pair(p):
        lanes = pl.ds(p * 128, 128)
        ind = ind_ref[:, lanes].astype(F32)
        ia = jnp.where(half_lane, ind, 0.0)
        ib = jnp.where(half_lane, 0.0, ind)
        bd = jnp.concatenate([ia] * nb + [ib] * nb, axis=0).astype(BF16)
        s = dg(kk[:, lanes], bd, NT) * 0.125
        b = bias[...]
        s = s + jnp.concatenate([b, b], axis=1)
        top = jnp.maximum(jnp.max(s, axis=0, keepdims=True), -1e29)
        thi = top.astype(BF16).astype(F32)
        top = thi + (top - thi).astype(BF16).astype(F32)
        pr = jnp.exp(s - top)
        l = jnp.sum(pr, axis=0, keepdims=True)
        acc = dg(vv[:, lanes], pr.astype(BF16), TN)
        for h in range(2):
            hc = slice(h * 128, (h + 1) * 128)
            sbuf[h, p, 0:HD] = acc[h * HD:(h + 1) * HD, hc]
            sbuf[h, p, HD:HD + 8] = jnp.where(
                row8 == 0, top[:, hc], jnp.where(row8 == 1, l[:, hc], 0.0)
            )

    for half in range(2):
        own = range(half * pairs // 2, (half + 1) * pairs // 2)
        for p in own:
            partial_pair(p)
        for p in own:
            s1_copy(p).start()

    row16 = iota((16, 128), 0)

    def s2_copy(k):
        p = lax.rem(chip + k, chips)
        return pltpu.make_async_remote_copy(
            src_ref=msg.at[p], dst_ref=recv2.at[chip],
            send_sem=s2s.at[p], recv_sem=s2r.at[chip],
            device_id=peer(p * 2 + core), device_id_type=MESH,
        )

    def merge_pair(k):
        p = lax.rem(chip + k, chips)
        s1_copy(p).wait_recv()
        m0, m1 = sbuf[core, p, HD:HD + 1], s1recv[p, HD:HD + 1]
        l0, l1 = sbuf[core, p, HD + 1:HD + 2], s1recv[p, HD + 1:HD + 2]
        mx = jnp.maximum(m0, m1)
        f0, f1 = jnp.exp(m0 - mx), jnp.exp(m1 - mx)
        l = l0 * f0 + l1 * f1
        msg[p, 0:HD] = (sbuf[core, p, 0:HD] * f0 + s1recv[p, 0:HD] * f1).astype(BF16)
        mhi = mx.astype(BF16).astype(F32)
        lhi = l.astype(BF16).astype(F32)
        st = jnp.where(row16 == 0, mhi, jnp.where(row16 == 1, mx - mhi, 0.0))
        st = jnp.where(row16 == 2, lhi, jnp.where(row16 == 3, l - lhi, st))
        msg[p, HD:HD + 16] = st.astype(BF16)

    def merge_send(k, _):
        merge_pair(k)
        s2_copy(k).start()
        return 0

    lax.fori_loop(1, chips, merge_send, 0)
    merge_pair(0)

    loads[3 + tchunks].wait()
    project(wq, qq)
    loads[4 + tchunks].wait()

    def u_tile(j, _):
        rows = pl.ds(pl.multiple_of(j * 128, 128), 128)
        a = jnp.zeros((128, 128), F32)
        for c in range(width // 128):
            cs = slice(c * 128, (c + 1) * 128)
            a = a + wo[rows, cs].astype(F32) * sv_ref[:, cs]
        ubc[rows, :] = jnp.broadcast_to(jnp.sum(a, axis=1, keepdims=True), (128, 128))
        return 0

    lax.fori_loop(0, width // 128, u_tile, 0)
    esv = jnp.sum(enc[...].astype(F32) * sv_ref[...], axis=1, keepdims=True)
    esv_row = jnp.sum(jnp.where(cc == rr, esv, 0.0), axis=0, keepdims=True)

    def s2_wait(k, _):
        src = lax.rem(chip + k, chips)
        pltpu.make_async_remote_copy(
            src_ref=msg.at[src], dst_ref=recv2.at[src],
            send_sem=s2s.at[src], recv_sem=s2r.at[src],
            device_id=sibling, device_id_type=MESH,
        ).wait_recv()
        return 0

    lax.fori_loop(1, chips, s2_wait, 0)
    recv2[chip] = msg[chip]

    def stats(i):
        st = recv2[i, HD:HD + 16].astype(F32)
        return st[0:1] + st[1:2], st[2:3] + st[3:4]

    ml = [stats(i) for i in range(chips)]
    mx = functools.reduce(jnp.maximum, [m for m, _ in ml])
    acc = jnp.zeros((HD, 128), F32)
    lsum = jnp.zeros((1, 128), F32)
    for i in range(chips):
        f = jnp.exp(ml[i][0] - mx)
        lsum = lsum + ml[i][1] * f
        acc = acc + recv2[i, 0:HD].astype(F32) * f
    gath[chip, core] = (acc / lsum).astype(BF16)

    def ag_copy(k):
        return pltpu.make_async_remote_copy(
            src_ref=gath.at[chip, core], dst_ref=gath.at[chip, core],
            send_sem=ags.at[k], recv_sem=agr.at[chip],
            device_id=peer(lax.rem(chip + k, chips) * 2 + core), device_id_type=MESH,
        )

    def fw_copy(p):
        return pltpu.make_async_remote_copy(
            src_ref=gath.at[p, core], dst_ref=gath.at[p, core],
            send_sem=fws.at[p], recv_sem=fwr.at[p],
            device_id=sibling, device_id_type=MESH,
        )

    for k in range(1, chips):
        ag_copy(k).start()
    fw_copy(chip).start()

    def comp_wait(k, _):
        src = lax.rem(me + k, n)
        pltpu.make_async_remote_copy(
            src_ref=comp_all.at[src], dst_ref=comp_all.at[src],
            send_sem=cs_sem.at[k], recv_sem=cr_sem.at[src],
            device_id=sibling, device_id_type=MESH,
        ).wait_recv()
        return 0

    lax.fori_loop(1, n, comp_wait, 0)
    hrow = iota((hi_rows, cand), 0)
    lrow = iota((128, cand), 0)

    def valid_step(b, t):
        cr = comp_all[b]
        rm = jnp.where(lax.rem(cr, 128) == lrow, 1.0, 0.0).astype(BF16)
        rt[b] = rm
        return t + dg(jnp.where((cr // 128) == hrow, 1.0, 0.0).astype(BF16), rm, NT)

    valid = lax.fori_loop(0, n, valid_step, jnp.zeros((hi_rows, 128), F32))

    def forward_block(k, _):
        src = lax.rem(chip + k, chips)
        pltpu.make_async_remote_copy(
            src_ref=gath.at[src, core], dst_ref=gath.at[src, core],
            send_sem=ags.at[k], recv_sem=agr.at[src],
            device_id=sibling, device_id_type=MESH,
        ).wait_recv()
        fw_copy(src).start()
        return 0

    lax.fori_loop(1, chips, forward_block, 0)

    def fw_wait(p, _):
        pltpu.make_async_remote_copy(
            src_ref=gath.at[p, 1 - core], dst_ref=gath.at[p, 1 - core],
            send_sem=fws.at[p], recv_sem=fwr.at[p],
            device_id=sibling, device_id_type=MESH,
        ).wait_recv()
        return 0

    lax.fori_loop(0, chips, fw_wait, 0)

    masks = [slate_row == float(s) for s in range(nb)]
    half_row = iota((128, 128), 0) < HD

    def block_diag(p):
        g = jnp.concatenate([gath[p, 0], gath[p, 1]], axis=0).astype(F32)
        return jnp.concatenate(
            [jnp.where(half_row, g, 0.0), jnp.where(half_row, 0.0, g)], axis=1
        ).astype(BF16)

    def pick(z):
        r = z[0:INDUCE]
        for s in range(1, nb):
            r = jnp.where(masks[s], z[s * INDUCE:(s + 1) * INDUCE], r)
        return r

    def spread(a, b):
        return jnp.concatenate(
            [jnp.where(m, a, 0.0) for m in masks] + [jnp.where(m, b, 0.0) for m in masks], axis=0
        ).astype(BF16)

    def wide(x):
        return jnp.concatenate([x] * (cand // 128), axis=1)

    def score_pair(p, row):
        lanes = pl.ds(p * 128, 128)
        bd = block_diag(p)
        z = dg(bd, qq[:, lanes], (((0,), (1,)), ((), ())))
        ws = []
        for h in range(2):
            zs = pick(z[h * 128:(h + 1) * 128]) * 0.125
            e = jnp.exp(zs - jnp.max(zs, axis=0, keepdims=True))
            w = e / jnp.sum(e, axis=0, keepdims=True)
            prob[p, h * INDUCE:(h + 1) * INDUCE] = w
            ws.append(w)
        mix = jnp.dot(bd, spread(ws[0], ws[1]), preferred_element_type=F32)
        u = wide(ubc[lanes, :])
        mu = mix * u
        sa = jnp.sum(mu[0:HD], axis=0, keepdims=True)
        sb = jnp.sum(mu[HD:2 * HD], axis=0, keepdims=True)
        r8 = iota((8, cand), 0)
        srow[p] = jnp.where(r8 == 0, sa, sb)
        return row + jnp.sum(mix.astype(BF16).astype(F32) * u, axis=0, keepdims=True)

    score_row = esv_row
    for p in range(pairs):
        score_row = score_pair(p, score_row)
    sc_all[me] = score_row
    sc_sends = []
    for k in range(1, n):
        c = pltpu.make_async_remote_copy(
            src_ref=sc_all.at[me], dst_ref=sc_all.at[me],
            send_sem=ss_sem.at[k], recv_sem=sr_sem.at[me],
            device_id=peer(lax.rem(me + k, n)), device_id_type=MESH,
        )
        c.start()
        sc_sends.append(c)

    def back_pair(p):
        lanes = pl.ds(p * 128, 128)
        bd = block_diag(p)
        u = ubc[lanes, :]
        uh = u.astype(BF16)
        ul = (u - uh.astype(F32)).astype(BF16)
        t = wide(dg(bd, uh, TN) + dg(bd, ul, TN))
        ds = []
        for h in range(2):
            ts = pick(t[h * 128:(h + 1) * 128])
            ds.append(prob[p, h * INDUCE:(h + 1) * INDUCE] * (ts - srow[p, h:h + 1]) * 0.125)
        dq[lanes, :] = jnp.dot(bd, spread(ds[0], ds[1]), preferred_element_type=F32).astype(BF16)

    for p in range(pairs):
        back_pair(p)

    def b_tile(cols):
        y = jnp.dot(wq[cols, :], dq[...], preferred_element_type=F32)
        bb[:, cols] = jnp.transpose(y) + sv_ref[:, cols]

    tiles(b_tile)
    bb_out = pltpu.make_async_copy(bb, bb_hbm, out_sem)
    bb_out.start()

    def sc_wait(k, _):
        src = lax.rem(me + k, n)
        pltpu.make_async_remote_copy(
            src_ref=sc_all.at[src], dst_ref=sc_all.at[src],
            send_sem=ss_sem.at[k], recv_sem=sr_sem.at[src],
            device_id=sibling, device_id_type=MESH,
        ).wait_recv()
        return 0

    lax.fori_loop(1, n, sc_wait, 0)

    per = hi_rows // nb
    prow = iota((per, cand), 0)
    spots = jnp.zeros((2 * per, 128), F32)
    ssum = jnp.zeros((1, cand), F32)
    for b in range(n):
        cr, sc = comp_all[b], sc_all[b]
        e = jnp.exp(sc)
        eh = e.astype(BF16).astype(F32)
        at = lax.rem(cr, total) // 128 == prow
        both = jnp.concatenate([jnp.where(at, eh, 0.0), jnp.where(at, e - eh, 0.0)], axis=0)
        spots = spots + dg(both.astype(BF16), rt[b], NT)
        ssum = ssum + jnp.where((cr // total) == mybin, sc, 0.0)
    is_valid = valid > 0.5
    table = jnp.where(is_valid, jnp.concatenate([spots[0:per] + spots[per:]] * nb, axis=0), 0.0)

    ri, ci = iota((128, 128), 0), iota((128, 128), 1)
    same = (ri // per) == (ci // per)

    def ones_where(m):
        return jnp.where(m, 1.0, 0.0).astype(BF16)

    def split(x, axis):
        hi = x.astype(BF16)
        return jnp.concatenate([hi, (x - hi.astype(F32)).astype(BF16)], axis=axis)

    def scan_keys(x, within, across):
        y = jnp.dot(split(x, 0), within, preferred_element_type=F32)
        y = y[0:hi_rows] + y[hi_rows:]
        z = jnp.dot(across, split(y[:, 128:], 1), preferred_element_type=F32)
        return y[:, 0:128] + z[:, 0:128] + z[:, 128:]

    all_ones = jnp.ones((128, 128), BF16)
    suf = jnp.concatenate([ones_where(ri >= ci), all_ones], axis=1)
    pre = jnp.concatenate([ones_where(ri <= ci), all_ones], axis=1)
    later = ones_where(same & (ci > ri))
    earlier = ones_where(same & (ci < ri))

    den = scan_keys(table, suf, later)
    den = jnp.where(is_valid, den, 1.0)
    ln = jnp.where(is_valid & ((ri // per) == mybin), jnp.log(den), 0.0)
    loss_ref[0] = jnp.sum(ln) - jnp.sum(ssum)
    inv = jnp.where(is_valid, 1.0 / den, 0.0)
    acc2 = scan_keys(inv, pre, earlier)
    lc = ones_where((comp_col // 128) == iota((cand, hi_rows), 1))
    mine = jnp.dot(lc, split(acc2, 1), preferred_element_type=F32)
    mine = mine[:, 0:128] + mine[:, 128:]
    mine = jnp.where(lax.rem(comp_col, 128) == iota((cand, 128), 1), mine, 0.0)
    acc_col = jnp.sum(mine, axis=1, keepdims=True)
    e_col = jnp.exp(jnp.sum(jnp.where(cc == rr, score_row, 0.0), axis=1, keepdims=True))
    g = e_col * acc_col - 1.0
    g_ref[...] = jnp.broadcast_to(g, (cand, 128))
    bb_out.wait()

    for c in comp_sends + sc_sends:
        c.wait_send()
    for p in range(pairs):
        s1_copy(p).wait_send()
        fw_copy(p).wait_send()
    for k in range(1, chips):
        s2_copy(k).wait_send()
        ag_copy(k).wait_send()


def fused(
    tokens, enc_gain, enc_weight, lengths, membership, target_keys,
    key_weight, value_weight, query_weight, out_weight, inducing, score_vector,
):
    ntok, width = tokens.shape
    cand = membership.shape[0]
    n = 16
    any_spec = pl.BlockSpec(memory_space=pl.ANY)
    vm = pl.BlockSpec(memory_space=pltpu.VMEM)
    dma = pltpu.SemaphoreType.DMA
    mat = pltpu.VMEM((width, width), BF16)
    rows = pltpu.VMEM((cand, width), BF16)
    back, grad, loss = pl.pallas_call(
        fused_kernel,
        out_shape=(
            jax.ShapeDtypeStruct((cand, width), F32),
            jax.ShapeDtypeStruct((cand, 128), F32),
            jax.ShapeDtypeStruct((1,), F32),
        ),
        in_specs=[any_spec] * 6 + [vm] * 6,
        out_specs=(any_spec, vm, pl.BlockSpec(memory_space=pltpu.SMEM)),
        scratch_shapes=[
            pltpu.VMEM((ntok, width), BF16), mat, mat, mat, mat, mat,
            pltpu.VMEM((ntok, width), BF16), pltpu.VMEM((cand, ntok), BF16),
            rows, rows, rows, rows, pltpu.VMEM((cand, 128), F32),
            pltpu.VMEM((2, 8, HD + 8, 128), F32), pltpu.VMEM((8, HD + 8, 128), F32),
            pltpu.VMEM((8, HD + 16, 128), BF16), pltpu.VMEM((8, HD + 16, 128), BF16),
            pltpu.VMEM((8, 2, HD, 128), BF16), pltpu.VMEM((width, 128), F32),
            pltpu.VMEM((8, 2 * INDUCE, cand), F32), pltpu.VMEM((8, 8, cand), F32),
            pltpu.VMEM((width, cand), BF16), pltpu.VMEM((cand, width), F32),
            pltpu.VMEM((n, 1, cand), jnp.int32), pltpu.VMEM((n, 1, cand), F32),
            dma((5 + ntok // 256,)), dma((n,)), dma((n,)), dma((n,)), dma((n,)),
            dma((8,)), dma((8,)), dma((8,)), dma((8,)), dma((8,)), dma((8,)), dma((8,)), dma((8,)),
            dma, pltpu.VMEM((n, 128, cand), BF16),
        ],
        compiler_params=pltpu.CompilerParams(
            collective_id=0, has_side_effects=True, vmem_limit_bytes=56 * 1024 * 1024
        ),
        cost_estimate=pl.CostEstimate(
            flops=8_000_000_000, bytes_accessed=13_000_000, transcendentals=1_000_000
        ),
    )(
        tokens, enc_weight, key_weight, value_weight, query_weight, out_weight,
        enc_gain.reshape(1, width), lengths, membership.reshape(1, cand), target_keys.reshape(1, cand),
        inducing, score_vector.reshape(1, width),
    )
    return (back * grad[:, :1]).astype(BF16), loss


def solution(mesh):
    placed = (
        P(("groups", "bins", "blk"), None),
        P(),
        P(),
        P(("groups", "bins", "blk"), None),
        P(("groups", "bins", "blk"), None),
        P(("groups", "bins", "blk")),
        P(),
        P(),
        P(),
        P(),
        P(),
        P(),
    )
    small = mesh.shape["bins"] == 4 and mesh.shape["blk"] == 4
    return jax.shard_map(
        fused if small else local,
        mesh=mesh,
        in_specs=placed,
        out_specs=(P(("groups", "bins", "blk"), None), P(("groups", "bins"))),
        check_vma=False,
    )
```

```python
import functools

import jax
import jax.numpy as jnp
from jax import lax
from jax.experimental import pallas as pl
from jax.experimental.pallas import tpu as pltpu
from jax.sharding import PartitionSpec as P

HEADS = 16
HD = 64
INDUCE = 32


def fold_induced(carry, keys_piece, values_piece, valid_piece, inducing):
    run_max, run_sum, run_acc = carry
    count = keys_piece.shape[0]
    head_keys = keys_piece.reshape(count, HEADS, HD)
    head_vals = values_piece.reshape(count, HEADS, HD).astype(jnp.float32)
    queries = inducing.reshape(INDUCE, HEADS, HD)
    scores = jnp.einsum(
        "ihd,nhd->hin", queries, head_keys, preferred_element_type=jnp.float32
    ) / jnp.sqrt(jnp.float32(HD))
    usable = valid_piece > 0
    scores = jnp.where(usable[None, None, :], scores, -1e30)
    new_max = jnp.maximum(run_max, jnp.max(scores, axis=-1))
    probs = jnp.where(usable[None, None, :], jnp.exp(scores - new_max[..., None]), 0.0)
    new_sum = jnp.sum(probs, axis=-1)
    new_acc = jnp.einsum("hin,nhd->hid", probs, head_vals)
    return (new_max, new_sum, new_acc)


def doc_scores(rows_f, induced, query_weight, out_weight, score_vector):
    count = rows_f.shape[0]
    rows_b = rows_f.astype(jnp.bfloat16)
    quer = jnp.dot(rows_b, query_weight, preferred_element_type=jnp.float32).astype(jnp.bfloat16)
    quer = quer.reshape(count, HEADS, HD)
    head_ind = induced.reshape(INDUCE, HEADS, HD)
    scores = jnp.einsum(
        "nhd,jhd->nhj", quer, head_ind, preferred_element_type=jnp.float32
    ) / jnp.sqrt(jnp.float32(HD))
    weights = jax.nn.softmax(scores, axis=-1).astype(jnp.bfloat16)
    mixed = jnp.einsum("nhj,jhd->nhd", weights, head_ind, preferred_element_type=jnp.float32)
    mixed = mixed.reshape(count, HEADS * HD).astype(jnp.bfloat16)
    full = rows_f + jnp.dot(mixed, out_weight, preferred_element_type=jnp.float32)
    return jnp.sum(full * score_vector, axis=-1)


def local(
    tokens,
    enc_gain,
    enc_weight,
    lengths,
    membership,
    target_keys,
    key_weight,
    value_weight,
    query_weight,
    out_weight,
    inducing,
    score_vector,
):
    tok_count = tokens.shape[0]
    xf = tokens.astype(jnp.float32)
    meansq = jnp.mean(xf * xf, axis=-1, keepdims=True)
    normed = (xf * lax.rsqrt(meansq + 1e-06) * enc_gain).astype(jnp.bfloat16)
    enc_tok = (xf + jnp.dot(normed, enc_weight, preferred_element_type=jnp.float32)).astype(
        jnp.bfloat16
    )
    lens = lengths[0]
    cand = lens.shape[0]
    seq = jnp.arange(cand, dtype=jnp.int32)
    ends = jnp.sum(jnp.where(seq[None, :] <= seq[:, None], lens[None, :], 0), axis=1)
    starts = ends - lens
    position = jnp.arange(tok_count, dtype=jnp.int32)
    member_tok = (position[None, :] >= starts[:, None]) & (position[None, :] < ends[:, None])
    pooled = jnp.dot(member_tok.astype(jnp.bfloat16), enc_tok, preferred_element_type=jnp.float32)
    encoded = (pooled / lens[:, None].astype(jnp.float32)).astype(jnp.bfloat16)
    nbins = lax.axis_size("bins")
    slots = max(2, 5 * cand // (4 * nbins))
    total_slots = nbins * slots
    dest = membership[:, 0]
    order = jnp.arange(cand, dtype=jnp.int32)
    same_dest = (dest[:, None] == dest[None, :]) & (order[:, None] > order[None, :])
    rank = jnp.sum(same_dest.astype(jnp.int32), axis=1)
    slot_of = dest * slots + rank
    placed = jnp.arange(total_slots, dtype=jnp.int32)[:, None] == slot_of[None, :]
    placed_b = placed.astype(jnp.bfloat16)
    send_rows = jnp.dot(placed_b, encoded, preferred_element_type=jnp.float32).astype(jnp.bfloat16)
    send_tags = jnp.sum(jnp.where(placed, target_keys[None, :] + 1, 0), axis=1)
    width = encoded.shape[1]
    slate_rows = lax.all_to_all(
        send_rows.reshape(nbins, slots, width), "bins", split_axis=0, concat_axis=0, tiled=True
    ).reshape(total_slots, width)
    tags = lax.all_to_all(
        send_tags.reshape(nbins, slots), "bins", split_axis=0, concat_axis=0, tiled=True
    ).reshape(total_slots)
    valid = tags > 0
    valid_b = valid.astype(jnp.bfloat16)
    keys = jnp.dot(slate_rows, key_weight, preferred_element_type=jnp.float32).astype(jnp.bfloat16)
    values = jnp.dot(slate_rows, value_weight, preferred_element_type=jnp.float32).astype(
        jnp.bfloat16
    )
    start_state = (
        jnp.full((HEADS, INDUCE), -1e30, jnp.float32),
        jnp.zeros((HEADS, INDUCE), jnp.float32),
        jnp.zeros((HEADS, INDUCE, HD), jnp.float32),
    )
    state = fold_induced(
        start_state,
        lax.all_gather(keys, "blk", axis=0, tiled=True),
        lax.all_gather(values, "blk", axis=0, tiled=True),
        lax.all_gather(valid_b, "blk", axis=0, tiled=True),
        inducing,
    )
    induced = state[2] / state[1][..., None]
    induced = jnp.transpose(induced, (1, 0, 2)).reshape(INDUCE, HEADS * HD).astype(jnp.bfloat16)
    rows_f = slate_rows.astype(jnp.float32)
    score, pull = jax.vjp(
        lambda rows: doc_scores(rows, induced, query_weight, out_weight, score_vector), rows_f
    )
    expo = jnp.where(valid, jnp.exp(score), 0.0)
    tag_f = tags.astype(jnp.float32)
    other_tags = lax.all_gather(tag_f, "blk", axis=0, tiled=True)
    other_exp = lax.all_gather(expo, "blk", axis=0, tiled=True)
    keep = other_tags[None, :] >= tag_f[:, None]
    den = jnp.sum(jnp.where(keep, other_exp[None, :], 0.0), axis=1)
    den_safe = jnp.where(valid, den, 1.0)
    loss_rows = jnp.where(valid, jnp.log(den_safe) - score, 0.0)
    slate_loss = lax.psum(jnp.sum(loss_rows), "blk")
    inverse = jnp.where(valid, 1.0 / den_safe, 0.0)
    other_tags = lax.all_gather(tag_f, "blk", axis=0, tiled=True)
    other_inv = lax.all_gather(inverse, "blk", axis=0, tiled=True)
    keep = other_tags[None, :] <= tag_f[:, None]
    acc_inv = jnp.sum(jnp.where(keep, other_inv[None, :], 0.0), axis=1)
    score_grad = jnp.where(valid, expo * acc_inv - 1.0, 0.0)
    slot_grads = pull(score_grad)[0].astype(jnp.bfloat16)
    returned = lax.all_to_all(
        slot_grads.reshape(nbins, slots, width), "bins", split_axis=0, concat_axis=0, tiled=True
    ).reshape(total_slots, width)
    row_grads = jnp.einsum(
        "sc,sd->cd", placed_b, returned, preferred_element_type=jnp.float32
    ).astype(jnp.bfloat16)
    return (row_grads, jnp.reshape(slate_loss, (1,)))


MESH = pl.DeviceIdType.MESH
F32 = jnp.float32
BF16 = jnp.bfloat16
NEG = -1e30
NT = (((1,), (1,)), ((), ()))
TN = (((0,), (0,)), ((), ()))


def dg(a, b, dims):
    return lax.dot_general(a, b, dims, preferred_element_type=F32)


def iota(shape, axis):
    return lax.broadcasted_iota(jnp.int32, shape, axis)


def fused_kernel(
    tok_hbm, we_hbm, wk_hbm, wv_hbm, wq_hbm, wo_hbm,
    gain_ref, lens_ref, mem_ref, keys_ref, ind_ref, sv_ref,
    out_ref, loss_ref,
    tok, we, wk, wv, wq, wo, etok, pool, enc, kk, vv, qq, bias,
    sbuf, s1recv, msg, recv2, gath, ubc, prob, srow, dq, bb,
    comp_all, sc_all,
    ld_sem, cs_sem, cr_sem, ss_sem, sr_sem, s1s, s1r, s2s, s2r, ags, agr, fws, fwr,
    rt,
):
    nb, nk = 4, 4
    n = nb * nk
    width = tok.shape[1]
    cand = mem_ref.shape[1]
    ntok = tok.shape[0]
    total = n * cand
    hi_rows = nb * total // 128
    chips = n // 2
    pairs = HEADS // 2
    tile = 256
    mybin, myblk = lax.axis_index("bins"), lax.axis_index("blk")
    me = mybin * nk + myblk
    core = lax.rem(myblk, 2)
    chip = me // 2

    def peer(rank):
        return {"bins": rank // nk, "blk": lax.rem(rank, nk)}

    sibling = peer(chip * 2 + 1 - core)

    barrier = pltpu.get_barrier_semaphore()
    for k in range(1, n):
        pl.semaphore_signal(barrier, inc=1, device_id=peer(lax.rem(me + k, n)), device_id_type=MESH)

    tchunks = ntok // tile
    loads = [pltpu.make_async_copy(we_hbm, we, ld_sem.at[0])]
    for k in range(tchunks):
        loads.append(
            pltpu.make_async_copy(
                tok_hbm.at[pl.ds(k * tile, tile)], tok.at[pl.ds(k * tile, tile)], ld_sem.at[5 + k]
            )
        )
    loads.append(pltpu.make_async_copy(wk_hbm, wk, ld_sem.at[1]))
    loads.append(pltpu.make_async_copy(wv_hbm, wv, ld_sem.at[2]))
    loads.append(pltpu.make_async_copy(wq_hbm, wq, ld_sem.at[3]))
    loads.append(pltpu.make_async_copy(wo_hbm, wo, ld_sem.at[4]))
    for c in loads[: 1 + tchunks]:
        c.start()

    rr, cc = iota((cand, cand), 0), iota((cand, cand), 1)
    lens_row = lens_ref[...].astype(F32)
    ends = jnp.sum(jnp.where(cc <= rr, lens_row, 0.0), axis=1, keepdims=True)
    lens_col = jnp.sum(jnp.where(cc == rr, lens_row, 0.0), axis=1, keepdims=True)
    starts = ends - lens_col
    pos = iota((cand, ntok), 1).astype(F32)
    pool[...] = jnp.where((pos >= starts) & (pos < ends), 1.0, 0.0).astype(BF16)
    inv_len = lens_col
    slate_row = mem_ref[...].astype(F32)
    slate_col = jnp.sum(jnp.where(cc == rr, slate_row, 0.0), axis=1, keepdims=True)
    key_row = keys_ref[...].astype(F32)
    key_col = jnp.sum(jnp.where(cc == rr, key_row, 0.0), axis=1, keepdims=True)
    comp_row = (slate_row * float(total) + key_row).astype(jnp.int32)
    comp_col = (slate_col * float(total) + key_col).astype(jnp.int32)
    comp_all[me] = comp_row
    lane_slate = (iota((cand, 128), 1) // INDUCE).astype(F32)
    bias[...] = jnp.where(lane_slate == slate_col, 0.0, NEG)

    pl.semaphore_wait(barrier, n - 1)
    comp_sends = []
    for k in range(1, n):
        c = pltpu.make_async_remote_copy(
            src_ref=comp_all.at[me], dst_ref=comp_all.at[me],
            send_sem=cs_sem.at[k], recv_sem=cr_sem.at[me],
            device_id=peer(lax.rem(me + k, n)), device_id_type=MESH,
        )
        c.start()
        comp_sends.append(c)

    loads[0].wait()
    loads[1 + tchunks].start()
    loads[2 + tchunks].start()

    for k in range(tchunks):
        rows = pl.ds(k * tile, tile)
        loads[1 + k].wait()
        x = tok[rows, :].astype(F32)
        ms = jnp.mean(x * x, axis=-1, keepdims=True)
        normed = (x * lax.rsqrt(ms + 1e-06) * gain_ref[...]).astype(BF16)
        for j in range(width // tile):
            cols = pl.ds(j * tile, tile)
            y = tok[rows, cols].astype(F32) + jnp.dot(
                normed, we[:, cols], preferred_element_type=F32
            )
            etok[rows, cols] = y.astype(BF16)

    loads[3 + tchunks].start()
    loads[4 + tchunks].start()

    def tiles(body):
        for j in range(width // tile):
            body(pl.ds(j * tile, tile))

    def pool_tile(cols):
        y = jnp.dot(pool[...], etok[:, cols], preferred_element_type=F32)
        enc[:, cols] = (y / inv_len).astype(BF16)

    tiles(pool_tile)

    def project(w, dst):
        def body(cols):
            dst[:, cols] = jnp.dot(enc[...], w[:, cols], preferred_element_type=F32).astype(BF16)

        tiles(body)

    loads[1 + tchunks].wait()
    project(wk, kk)
    loads[2 + tchunks].wait()
    project(wv, vv)

    row8 = iota((8, 128), 0)
    half_lane = iota((INDUCE, 128), 1) < HD

    def s1_copy(p):
        return pltpu.make_async_remote_copy(
            src_ref=sbuf.at[1 - core, p], dst_ref=s1recv.at[p],
            send_sem=s1s.at[p], recv_sem=s1r.at[p],
            device_id=sibling, device_id_type=MESH,
        )

    def partial_pair(p):
        lanes = pl.ds(p * 128, 128)
        ind = ind_ref[:, lanes].astype(F32)
        ia = jnp.where(half_lane, ind, 0.0)
        ib = jnp.where(half_lane, 0.0, ind)
        bd = jnp.concatenate([ia] * nb + [ib] * nb, axis=0).astype(BF16)
        s = dg(kk[:, lanes], bd, NT) * 0.125
        b = bias[...]
        s = s + jnp.concatenate([b, b], axis=1)
        top = jnp.maximum(jnp.max(s, axis=0, keepdims=True), -1e29)
        thi = top.astype(BF16).astype(F32)
        top = thi + (top - thi).astype(BF16).astype(F32)
        pr = jnp.exp(s - top)
        l = jnp.sum(pr, axis=0, keepdims=True)
        acc = dg(vv[:, lanes], pr.astype(BF16), TN)
        for h in range(2):
            hc = slice(h * 128, (h + 1) * 128)
            sbuf[h, p, 0:HD] = acc[h * HD:(h + 1) * HD, hc]
            sbuf[h, p, HD:HD + 8] = jnp.where(
                row8 == 0, top[:, hc], jnp.where(row8 == 1, l[:, hc], 0.0)
            )

    for half in range(2):
        own = range(half * pairs // 2, (half + 1) * pairs // 2)
        for p in own:
            partial_pair(p)
        for p in own:
            s1_copy(p).start()

    row16 = iota((16, 128), 0)

    def s2_copy(k):
        p = lax.rem(chip + k, chips)
        return pltpu.make_async_remote_copy(
            src_ref=msg.at[p], dst_ref=recv2.at[chip],
            send_sem=s2s.at[p], recv_sem=s2r.at[chip],
            device_id=peer(p * 2 + core), device_id_type=MESH,
        )

    def merge_pair(k):
        p = lax.rem(chip + k, chips)
        s1_copy(p).wait_recv()
        m0, m1 = sbuf[core, p, HD:HD + 1], s1recv[p, HD:HD + 1]
        l0, l1 = sbuf[core, p, HD + 1:HD + 2], s1recv[p, HD + 1:HD + 2]
        mx = jnp.maximum(m0, m1)
        f0, f1 = jnp.exp(m0 - mx), jnp.exp(m1 - mx)
        l = l0 * f0 + l1 * f1
        msg[p, 0:HD] = (sbuf[core, p, 0:HD] * f0 + s1recv[p, 0:HD] * f1).astype(BF16)
        mhi = mx.astype(BF16).astype(F32)
        lhi = l.astype(BF16).astype(F32)
        st = jnp.where(row16 == 0, mhi, jnp.where(row16 == 1, mx - mhi, 0.0))
        st = jnp.where(row16 == 2, lhi, jnp.where(row16 == 3, l - lhi, st))
        msg[p, HD:HD + 16] = st.astype(BF16)

    def merge_send(k, _):
        merge_pair(k)
        s2_copy(k).start()
        return 0

    lax.fori_loop(1, chips, merge_send, 0)
    merge_pair(0)

    loads[3 + tchunks].wait()
    project(wq, qq)
    loads[4 + tchunks].wait()

    def u_tile(j, _):
        rows = pl.ds(pl.multiple_of(j * 128, 128), 128)
        a = jnp.zeros((128, 128), F32)
        for c in range(width // 128):
            cs = slice(c * 128, (c + 1) * 128)
            a = a + wo[rows, cs].astype(F32) * sv_ref[:, cs]
        ubc[rows, :] = jnp.broadcast_to(jnp.sum(a, axis=1, keepdims=True), (128, 128))
        return 0

    lax.fori_loop(0, width // 128, u_tile, 0)
    esv = jnp.sum(enc[...].astype(F32) * sv_ref[...], axis=1, keepdims=True)
    esv_row = jnp.sum(jnp.where(cc == rr, esv, 0.0), axis=0, keepdims=True)

    def s2_wait(k, _):
        src = lax.rem(chip + k, chips)
        pltpu.make_async_remote_copy(
            src_ref=msg.at[src], dst_ref=recv2.at[src],
            send_sem=s2s.at[src], recv_sem=s2r.at[src],
            device_id=sibling, device_id_type=MESH,
        ).wait_recv()
        return 0

    lax.fori_loop(1, chips, s2_wait, 0)
    recv2[chip] = msg[chip]

    def stats(i):
        st = recv2[i, HD:HD + 16].astype(F32)
        return st[0:1] + st[1:2], st[2:3] + st[3:4]

    ml = [stats(i) for i in range(chips)]
    mx = functools.reduce(jnp.maximum, [m for m, _ in ml])
    acc = jnp.zeros((HD, 128), F32)
    lsum = jnp.zeros((1, 128), F32)
    for i in range(chips):
        f = jnp.exp(ml[i][0] - mx)
        lsum = lsum + ml[i][1] * f
        acc = acc + recv2[i, 0:HD].astype(F32) * f
    gath[chip, core] = (acc / lsum).astype(BF16)

    def ag_copy(k):
        return pltpu.make_async_remote_copy(
            src_ref=gath.at[chip, core], dst_ref=gath.at[chip, core],
            send_sem=ags.at[k], recv_sem=agr.at[chip],
            device_id=peer(lax.rem(chip + k, chips) * 2 + core), device_id_type=MESH,
        )

    def fw_copy(p):
        return pltpu.make_async_remote_copy(
            src_ref=gath.at[p, core], dst_ref=gath.at[p, core],
            send_sem=fws.at[p], recv_sem=fwr.at[p],
            device_id=sibling, device_id_type=MESH,
        )

    for k in range(1, chips):
        ag_copy(k).start()
    fw_copy(chip).start()

    def comp_wait(k, _):
        src = lax.rem(me + k, n)
        pltpu.make_async_remote_copy(
            src_ref=comp_all.at[src], dst_ref=comp_all.at[src],
            send_sem=cs_sem.at[k], recv_sem=cr_sem.at[src],
            device_id=sibling, device_id_type=MESH,
        ).wait_recv()
        return 0

    lax.fori_loop(1, n, comp_wait, 0)
    hrow = iota((hi_rows, cand), 0)
    lrow = iota((128, cand), 0)

    def valid_step(b, t):
        cr = comp_all[b]
        rm = jnp.where(lax.rem(cr, 128) == lrow, 1.0, 0.0).astype(BF16)
        rt[b] = rm
        return t + dg(jnp.where((cr // 128) == hrow, 1.0, 0.0).astype(BF16), rm, NT)

    valid = lax.fori_loop(0, n, valid_step, jnp.zeros((hi_rows, 128), F32))

    def forward_block(k, _):
        src = lax.rem(chip + k, chips)
        pltpu.make_async_remote_copy(
            src_ref=gath.at[src, core], dst_ref=gath.at[src, core],
            send_sem=ags.at[k], recv_sem=agr.at[src],
            device_id=sibling, device_id_type=MESH,
        ).wait_recv()
        fw_copy(src).start()
        return 0

    lax.fori_loop(1, chips, forward_block, 0)

    def fw_wait(p, _):
        pltpu.make_async_remote_copy(
            src_ref=gath.at[p, 1 - core], dst_ref=gath.at[p, 1 - core],
            send_sem=fws.at[p], recv_sem=fwr.at[p],
            device_id=sibling, device_id_type=MESH,
        ).wait_recv()
        return 0

    lax.fori_loop(0, chips, fw_wait, 0)

    masks = [slate_row == float(s) for s in range(nb)]
    half_row = iota((128, 128), 0) < HD

    def block_diag(p):
        g = jnp.concatenate([gath[p, 0], gath[p, 1]], axis=0).astype(F32)
        return jnp.concatenate(
            [jnp.where(half_row, g, 0.0), jnp.where(half_row, 0.0, g)], axis=1
        ).astype(BF16)

    def pick(z):
        r = z[0:INDUCE]
        for s in range(1, nb):
            r = jnp.where(masks[s], z[s * INDUCE:(s + 1) * INDUCE], r)
        return r

    def spread(a, b):
        return jnp.concatenate(
            [jnp.where(m, a, 0.0) for m in masks] + [jnp.where(m, b, 0.0) for m in masks], axis=0
        ).astype(BF16)

    def wide(x):
        return jnp.concatenate([x] * (cand // 128), axis=1)

    def score_pair(p, row):
        lanes = pl.ds(p * 128, 128)
        bd = block_diag(p)
        z = dg(bd, qq[:, lanes], (((0,), (1,)), ((), ())))
        ws = []
        for h in range(2):
            zs = pick(z[h * 128:(h + 1) * 128]) * 0.125
            e = jnp.exp(zs - jnp.max(zs, axis=0, keepdims=True))
            w = e / jnp.sum(e, axis=0, keepdims=True)
            prob[p, h * INDUCE:(h + 1) * INDUCE] = w
            ws.append(w)
        mix = jnp.dot(bd, spread(ws[0], ws[1]), preferred_element_type=F32)
        u = wide(ubc[lanes, :])
        mu = mix * u
        sa = jnp.sum(mu[0:HD], axis=0, keepdims=True)
        sb = jnp.sum(mu[HD:2 * HD], axis=0, keepdims=True)
        r8 = iota((8, cand), 0)
        srow[p] = jnp.where(r8 == 0, sa, sb)
        return row + jnp.sum(mix.astype(BF16).astype(F32) * u, axis=0, keepdims=True)

    score_row = esv_row
    for p in range(pairs):
        score_row = score_pair(p, score_row)
    sc_all[me] = score_row
    sc_sends = []
    for k in range(1, n):
        c = pltpu.make_async_remote_copy(
            src_ref=sc_all.at[me], dst_ref=sc_all.at[me],
            send_sem=ss_sem.at[k], recv_sem=sr_sem.at[me],
            device_id=peer(lax.rem(me + k, n)), device_id_type=MESH,
        )
        c.start()
        sc_sends.append(c)

    def back_pair(p):
        lanes = pl.ds(p * 128, 128)
        bd = block_diag(p)
        u = ubc[lanes, :]
        uh = u.astype(BF16)
        ul = (u - uh.astype(F32)).astype(BF16)
        t = wide(dg(bd, uh, TN) + dg(bd, ul, TN))
        ds = []
        for h in range(2):
            ts = pick(t[h * 128:(h + 1) * 128])
            ds.append(prob[p, h * INDUCE:(h + 1) * INDUCE] * (ts - srow[p, h:h + 1]) * 0.125)
        dq[lanes, :] = jnp.dot(bd, spread(ds[0], ds[1]), preferred_element_type=F32).astype(BF16)

    for p in range(pairs):
        back_pair(p)

    def b_tile(cols):
        y = jnp.dot(wq[cols, :], dq[...], preferred_element_type=F32)
        bb[:, cols] = jnp.transpose(y) + sv_ref[:, cols]

    tiles(b_tile)

    def sc_wait(k, _):
        src = lax.rem(me + k, n)
        pltpu.make_async_remote_copy(
            src_ref=sc_all.at[src], dst_ref=sc_all.at[src],
            send_sem=ss_sem.at[k], recv_sem=sr_sem.at[src],
            device_id=sibling, device_id_type=MESH,
        ).wait_recv()
        return 0

    lax.fori_loop(1, n, sc_wait, 0)

    per = hi_rows // nb
    prow = iota((per, cand), 0)
    spots = jnp.zeros((2 * per, 128), F32)
    ssum = jnp.zeros((1, cand), F32)
    for b in range(n):
        cr, sc = comp_all[b], sc_all[b]
        e = jnp.exp(sc)
        eh = e.astype(BF16).astype(F32)
        at = lax.rem(cr, total) // 128 == prow
        both = jnp.concatenate([jnp.where(at, eh, 0.0), jnp.where(at, e - eh, 0.0)], axis=0)
        spots = spots + dg(both.astype(BF16), rt[b], NT)
        ssum = ssum + jnp.where((cr // total) == mybin, sc, 0.0)
    is_valid = valid > 0.5
    table = jnp.where(is_valid, jnp.concatenate([spots[0:per] + spots[per:]] * nb, axis=0), 0.0)

    ri, ci = iota((128, 128), 0), iota((128, 128), 1)
    same = (ri // per) == (ci // per)

    def ones_where(m):
        return jnp.where(m, 1.0, 0.0).astype(BF16)

    def split(x, axis):
        hi = x.astype(BF16)
        return jnp.concatenate([hi, (x - hi.astype(F32)).astype(BF16)], axis=axis)

    def scan_keys(x, within, across):
        y = jnp.dot(split(x, 0), within, preferred_element_type=F32)
        y = y[0:hi_rows] + y[hi_rows:]
        z = jnp.dot(across, split(y[:, 128:], 1), preferred_element_type=F32)
        return y[:, 0:128] + z[:, 0:128] + z[:, 128:]

    all_ones = jnp.ones((128, 128), BF16)
    suf = jnp.concatenate([ones_where(ri >= ci), all_ones], axis=1)
    pre = jnp.concatenate([ones_where(ri <= ci), all_ones], axis=1)
    later = ones_where(same & (ci > ri))
    earlier = ones_where(same & (ci < ri))

    den = scan_keys(table, suf, later)
    den = jnp.where(is_valid, den, 1.0)
    ln = jnp.where(is_valid & ((ri // per) == mybin), jnp.log(den), 0.0)
    loss_ref[0] = jnp.sum(ln) - jnp.sum(ssum)
    inv = jnp.where(is_valid, 1.0 / den, 0.0)
    acc2 = scan_keys(inv, pre, earlier)
    lc = ones_where((comp_col // 128) == iota((cand, hi_rows), 1))
    mine = jnp.dot(lc, split(acc2, 1), preferred_element_type=F32)
    mine = mine[:, 0:128] + mine[:, 128:]
    mine = jnp.where(lax.rem(comp_col, 128) == iota((cand, 128), 1), mine, 0.0)
    acc_col = jnp.sum(mine, axis=1, keepdims=True)
    e_col = jnp.exp(jnp.sum(jnp.where(cc == rr, score_row, 0.0), axis=1, keepdims=True))
    g = e_col * acc_col - 1.0
    out_ref[...] = (bb[...] * g).astype(BF16)

    for c in comp_sends + sc_sends:
        c.wait_send()
    for p in range(pairs):
        s1_copy(p).wait_send()
        fw_copy(p).wait_send()
    for k in range(1, chips):
        s2_copy(k).wait_send()
        ag_copy(k).wait_send()


def fused(
    tokens, enc_gain, enc_weight, lengths, membership, target_keys,
    key_weight, value_weight, query_weight, out_weight, inducing, score_vector,
):
    ntok, width = tokens.shape
    cand = membership.shape[0]
    n = 16
    any_spec = pl.BlockSpec(memory_space=pl.ANY)
    vm = pl.BlockSpec(memory_space=pltpu.VMEM)
    dma = pltpu.SemaphoreType.DMA
    mat = pltpu.VMEM((width, width), BF16)
    rows = pltpu.VMEM((cand, width), BF16)
    out, loss = pl.pallas_call(
        fused_kernel,
        out_shape=(
            jax.ShapeDtypeStruct((cand, width), BF16),
            jax.ShapeDtypeStruct((1,), F32),
        ),
        in_specs=[any_spec] * 6 + [vm] * 6,
        out_specs=(vm, pl.BlockSpec(memory_space=pltpu.SMEM)),
        scratch_shapes=[
            pltpu.VMEM((ntok, width), BF16), mat, mat, mat, mat, mat,
            pltpu.VMEM((ntok, width), BF16), pltpu.VMEM((cand, ntok), BF16),
            rows, rows, rows, rows, pltpu.VMEM((cand, 128), F32),
            pltpu.VMEM((2, 8, HD + 8, 128), F32), pltpu.VMEM((8, HD + 8, 128), F32),
            pltpu.VMEM((8, HD + 16, 128), BF16), pltpu.VMEM((8, HD + 16, 128), BF16),
            pltpu.VMEM((8, 2, HD, 128), BF16), pltpu.VMEM((width, 128), F32),
            pltpu.VMEM((8, 2 * INDUCE, cand), F32), pltpu.VMEM((8, 8, cand), F32),
            pltpu.VMEM((width, cand), BF16), pltpu.VMEM((cand, width), F32),
            pltpu.VMEM((n, 1, cand), jnp.int32), pltpu.VMEM((n, 1, cand), F32),
            dma((5 + ntok // 256,)), dma((n,)), dma((n,)), dma((n,)), dma((n,)),
            dma((8,)), dma((8,)), dma((8,)), dma((8,)), dma((8,)), dma((8,)), dma((8,)), dma((8,)),
            pltpu.VMEM((n, 128, cand), BF16),
        ],
        compiler_params=pltpu.CompilerParams(
            collective_id=0, has_side_effects=True, vmem_limit_bytes=56 * 1024 * 1024
        ),
        cost_estimate=pl.CostEstimate(
            flops=8_000_000_000, bytes_accessed=13_000_000, transcendentals=1_000_000
        ),
    )(
        tokens, enc_weight, key_weight, value_weight, query_weight, out_weight,
        enc_gain.reshape(1, width), lengths, membership.reshape(1, cand), target_keys.reshape(1, cand),
        inducing, score_vector.reshape(1, width),
    )
    return out, loss


def solution(mesh):
    placed = (
        P(("groups", "bins", "blk"), None),
        P(),
        P(),
        P(("groups", "bins", "blk"), None),
        P(("groups", "bins", "blk"), None),
        P(("groups", "bins", "blk")),
        P(),
        P(),
        P(),
        P(),
        P(),
        P(),
    )
    small = mesh.shape["bins"] == 4 and mesh.shape["blk"] == 4
    return jax.shard_map(
        fused if small else local,
        mesh=mesh,
        in_specs=placed,
        out_specs=(P(("groups", "bins", "blk"), None), P(("groups", "bins"))),
        check_vma=False,
    )
```
